32 devices in a mesh: ping: 8 (over y, x, core), rng: 4 (over z).
Axes of the slice: x: 2, y: 2, z: 4, core: 2. Of those that a mesh axis runs over, the one named last changes fastest.
Arguments:
- echoes: bfloat16 [128, 2, 32, 8192], P('ping', None, None, 'rng'), may hold values from -36 to 36, as said below
- pairing: int32 [128, 2, 8], P('ping'), may hold values from 0 to 31, as said below
- footprint: int32 [8, 48], replicated, may hold values from 0 to 127, as said below
- counts: int32 [8], replicated, may hold values from 1 to 48, 128 in all
- offsets: int32 [8, 48], replicated, may hold values from -64 to 64
- earlier: bfloat16 [8, 2, 1024, 8192], P('ping', None, None, 'rng'), may hold values from -6 to 6
Outputs:
- image: bfloat16 [8, 2, 1024, 8192], P('ping', None, None, 'rng')
The draws below stay inside these ranges and needn't reach their ends.
Inputs may be any that keep to these rules, and one draw needn't show every extreme that they name: `echoes`: the samples of a ping's pairing[p, 1] channels are partly a turned copy of ping p - 1's pairing[p, 0] channels. `pairing`: for each ping the 16 channels of its two rows are all different. `footprint`: the first counts[t] entries of row t are the pings that see tile t; the 48 entries of a row are different pings, and no aligned block of 16 pings (the pings of one ping owner, starting at a multiple of 16) holds more than 6 of them. `counts`: they sum to 128.
All inputs are finite; a program needn't handle non-finite values.
Results may differ from the reference program's by a relative error of at most 0.0053.
Values may be sent and summed in bfloat16 or wider, within the bound.
No kernel may reach another device: no remote copies, remote signals or barrier semaphores. Data moves between devices by JAX's collectives and lax.ppermute only.
A program may use at most 192 MiB of HBM per device.

```python
import math
import jax
import jax.numpy as jnp
import numpy as np
from jax import lax

C = 32
K = 8
R = 8192
X = 1024
BAND = 64
MOST = 48
TILE_DEV = 1
PING_DEV = 16
PINGS = 128
TILES = 8
CAP = 6
N_PING = 8


def pairing_table(key):
    ping_keys = jax.random.split(jax.random.fold_in(key, 11), PINGS)
    orders = jax.vmap(lambda one_key: jax.random.permutation(one_key, C))(ping_keys)
    return jnp.stack([orders[:, :K], orders[:, K:2 * K]], axis=1).astype(jnp.int32)


def draw_pairing(key, part):
    return pairing_table(key)


def draw_echoes(key, part):
    table = pairing_table(key)
    root_key = jax.random.fold_in(key, 23)
    gain_low, gain_high = (0.3, 3.0)
    gains = jnp.exp(jax.random.uniform(jax.random.fold_in(root_key, 1), (C,), minval=math.log(gain_low), maxval=math.log(gain_high)))
    taper = 0.5 + jnp.arange(R, dtype=jnp.float32) / R
    sway = jax.random.uniform(jax.random.fold_in(root_key, 2), (PINGS,), minval=-1.0, maxval=1.0)

    def fresh_noise(one_key):
        return jnp.clip(jax.random.normal(one_key, (2, C, R)), -4.0, 4.0)
    opening = jnp.clip(fresh_noise(jax.random.fold_in(root_key, 3)), -6.0, 6.0)

    def advance(previous, inputs):
        ping_one, pair_ids, angle = inputs
        noise_now = fresh_noise(jax.random.fold_in(root_key, 100 + ping_one))
        source = previous[:, pair_ids[0], :]
        turned = angle * taper
        cos_turn = jnp.cos(turned)
        sin_turn = jnp.sin(turned)
        coherent = jnp.stack([source[0] * cos_turn - source[1] * sin_turn, source[0] * sin_turn + source[1] * cos_turn])
        current = noise_now.at[:, pair_ids[1], :].set(0.8 * coherent + 0.6 * noise_now[:, pair_ids[1], :])
        current = jnp.clip(current, -6.0, 6.0)
        return (current, current)
    steps_in = (jnp.arange(1, PINGS, dtype=jnp.int32), table[1:], sway[1:])
    closing, following = lax.scan(advance, opening, steps_in)
    whole = jnp.concatenate([opening[None], following], axis=0)
    return (whole * gains[None, None, :, None] * taper[None, None, None, :]).astype(jnp.bfloat16)


def draw_footprint(key, part):
    root_key = jax.random.fold_in(key, 37)

    def one_tile(tile_key):
        first_key, second_key = jax.random.split(tile_key)
        chosen = jax.random.permutation(first_key, N_PING * CAP)[:MOST]
        owner_ids = chosen // CAP
        rank_ids = chosen % CAP
        owner_keys = jax.random.split(second_key, N_PING)
        orders = jax.vmap(lambda one_key: jax.random.permutation(one_key, PING_DEV))(owner_keys)
        local_ids = orders[owner_ids, rank_ids]
        return (owner_ids * PING_DEV + local_ids).astype(jnp.int32)
    return jax.vmap(one_tile)(jax.random.split(root_key, TILES))


def set_ends(result, stream_key, least, largest):
    longest = result.shape.index(max(result.shape))
    spots = []
    for shift in (0, 1):
        where = [jax.random.randint(jax.random.fold_in(stream_key, axis), (), 0, length) for axis, length in enumerate(result.shape)]
        where[longest] = (where[longest] + shift) % result.shape[longest]
        spots.append(tuple(where))
    return result.at[spots[0]].set(least).at[spots[1]].set(largest)


def level_of(own_key, extent, shards, least, high):
    def one(dim, parts):
        heights = jax.random.uniform(jax.random.fold_in(jax.random.fold_in(own_key, 6), dim), (parts,), jnp.float32, least / len(shards), high / len(shards))
        return jnp.repeat(jnp.exp(heights), extent[dim] // parts).reshape((-1,) + (1,) * (len(extent) - dim - 1))

    gain = one(*shards[0])
    for cut in shards[1:]:
        gain = gain * one(*cut)
    return gain


def split_up(amount, total, reach, slope):
    loads = [(1 << 20) // math.isqrt(rank ** slope) + 1 for rank in range(2, amount + 1)]
    spare, holding = total - reach - (amount - 1), [1] * (amount - 1)
    while spare > 0:
        candidates = [i for i in range(amount - 1) if holding[i] < reach]
        pool, remaining = sum([loads[i] for i in candidates]), spare
        for i in candidates:
            extra = min(reach - holding[i], max(1, remaining * loads[i] // pool), spare)
            holding[i] = holding[i] + extra
            spare = spare - extra
    return np.array([reach] + holding)


def ragged(stream_key, number_of, total, reach, slope):
    if number_of == 2:
        one = jax.random.randint(stream_key, (), max(1, total - reach), min(reach, total - 1) + 1)
        return jnp.stack([one, total - one])
    lengths = jnp.asarray(split_up(number_of, total, reach, slope), jnp.int32)
    pairs = (number_of - 1) // 2
    giver, sink = lengths[1:1 + 2 * pairs:2], lengths[2:2 + 2 * pairs:2]
    margin = jnp.minimum(giver - 1, reach - sink)
    moved = jax.random.randint(jax.random.fold_in(stream_key, 1), (pairs,), 0, 1 << 20) % (margin + 1)
    lengths = lengths.at[1:1 + 2 * pairs:2].set(giver - moved).at[2:2 + 2 * pairs:2].set(sink + moved)
    return lengths[jax.random.permutation(jax.random.fold_in(stream_key, 2), number_of)]


def scatter_about(stream_key, dims, width, reach, cuts=(), held_as=jnp.bfloat16):
    entries = width * jax.random.normal(stream_key, dims, jnp.float32)
    if cuts:
        entries = entries * level_of(stream_key, dims, cuts, -0.22, 0.18)
    return jnp.clip(entries, -reach, reach).astype(held_as)


def setup_inputs(seed: int = 0) -> dict:
    key_list = jax.random.split(jax.random.key(seed), 7)
    echoes = draw_echoes(jax.random.fold_in(key_list[6], 71), 0)
    pairing = draw_pairing(jax.random.fold_in(key_list[6], 71), 0)
    footprint = draw_footprint(jax.random.fold_in(key_list[6], 71), 0)
    counts = ragged(key_list[3], TILES, TILES * MOST // 3, MOST, 2).astype(jnp.int32)
    offsets = set_ends(jax.random.randint(key_list[4], (TILES, MOST), -BAND, BAND + 1), jax.random.fold_in(key_list[4], 1), -BAND, BAND).astype(jnp.int32)
    earlier = scatter_about(key_list[5], (TILES, 2, X, R), 1.0, 6.0, ((0, 8), (3, 4)))
    return dict(echoes=echoes, pairing=pairing, footprint=footprint, counts=counts, offsets=offsets, earlier=earlier)


phase_modulus = 4099
small_value = 1e-06

def weight_matrix(tile_id, ping_ids, shift_ids, live_rows, tile_count):
    spacing = TILE_DEV * X // PING_DEV
    column = jnp.arange(MOST * 2 * C, dtype=jnp.int32)
    part_of = column // C % 2
    channel = column % C
    ping_cols = jnp.repeat(ping_ids, 2 * C)
    shift_cols = jnp.repeat(shift_ids, 2 * C)
    live_cols = jnp.repeat(live_rows, 2 * C)
    pixels = jnp.arange(X, dtype=jnp.int32)
    offset = tile_id * X - ping_cols * spacing - 2 * channel
    folded = jnp.remainder(pixels[:, None] + offset[None, :], phase_modulus)
    square = jnp.remainder(folded * folded, phase_modulus)
    phases = square.astype(jnp.float32) * (2.0 * math.pi / phase_modulus) + shift_cols.astype(jnp.float32)[None, :] * (math.pi / 4.0)
    scales = live_cols / jnp.sqrt(jnp.float32(C) * tile_count.astype(jnp.float32))
    cosine = jnp.cos(phases) * scales[None, :]
    sines = jnp.sin(phases) * scales[None, :]
    upper_rows = jnp.where(part_of[None, :] == 0, cosine, -sines)
    lower_rows = jnp.where(part_of[None, :] == 0, sines, cosine)
    return jnp.concatenate([upper_rows, lower_rows], axis=0).astype(jnp.bfloat16)

def reference(echoes, pairing, footprint, counts, offsets, earlier):
    front_rows = jnp.take_along_axis(echoes[:-1], pairing[1:, 0][:, None, :, None], axis=2).astype(jnp.float32)
    front_rows = jnp.concatenate([jnp.zeros((1,) + front_rows.shape[1:], jnp.float32), front_rows], axis=0)
    rear_rows = jnp.take_along_axis(echoes, pairing[:, 1][:, None, :, None], axis=2).astype(jnp.float32)
    cross_sum = lax.optimization_barrier(jnp.sum(front_rows[:, 0] * rear_rows[:, 1] - front_rows[:, 1] * rear_rows[:, 0], axis=(1, 2)))
    front_energy = lax.optimization_barrier(jnp.sum(front_rows * front_rows, axis=(1, 2, 3)))
    rear_energy = lax.optimization_barrier(jnp.sum(rear_rows * rear_rows, axis=(1, 2, 3)))
    increment = cross_sum / (jnp.sqrt(front_energy * rear_energy) + small_value)
    track_turn = jnp.cumsum(increment)
    cosine = jnp.cos(track_turn)[:, None, None]
    sines = jnp.sin(track_turn)[:, None, None]
    real_part = echoes[:, 0].astype(jnp.float32)
    imag_part = echoes[:, 1].astype(jnp.float32)
    corrected = jnp.stack([real_part * cosine + imag_part * sines, imag_part * cosine - real_part * sines], axis=1).astype(jnp.bfloat16)
    padded = jnp.pad(corrected, ((0, 0), (0, 0), (0, 0), (BAND, BAND)))

    def one_tile(tile_id):
        ping_ids = footprint[tile_id]
        shift_ids = offsets[tile_id]
        tile_count = counts[tile_id]

        def window_of(ping_one, offset_one):
            return lax.dynamic_slice_in_dim(padded[ping_one], BAND + offset_one, R, axis=2)
        window = jax.vmap(window_of)(ping_ids, shift_ids)
        live_rows = (jnp.arange(MOST, dtype=jnp.int32) < tile_count).astype(jnp.float32)
        weights = weight_matrix(tile_id, ping_ids, shift_ids, live_rows, tile_count)
        product = jnp.dot(weights.astype(jnp.float32), window.reshape(MOST * 2 * C, R).astype(jnp.float32), precision=lax.Precision.HIGHEST)
        return (earlier[tile_id].astype(jnp.float32) + product.reshape(2, X, R)).astype(jnp.bfloat16)
    return lax.map(one_tile, jnp.arange(TILES, dtype=jnp.int32))
```

```python
import functools
import math

import jax
import jax.numpy as jnp
import numpy as np
from jax import lax
from jax.experimental import pallas as pl
from jax.experimental.pallas import tpu as pltpu
from jax.sharding import PartitionSpec as P

C = 32
X = 1024
BAND = 64
MOST = 48
TILE_DEV = 1
PING_DEV = 16


phase_modulus = 4099
small_value = 1e-06


def passed_along(shard, axis, by):
    length = lax.axis_size(axis)
    pairs = [(i, i + by) for i in range(length) if 0 <= i + by < length]
    return lax.ppermute(shard, axis, pairs)


def prefix(shard, axis, combine, identity):
    length, position = (lax.axis_size(axis), lax.axis_index(axis))
    everything = lax.all_gather(shard, axis)
    start = jnp.broadcast_to(jnp.asarray(identity, shard.dtype), shard.shape)

    def step(k, before):
        reached = k < position
        new = combine(before, everything[k])
        return jnp.where(reached, new, before)

    return lax.fori_loop(0, length, step, start)


def with_halo(cells, sides, width):
    for axis, dim in sides:
        count = lax.axis_size(axis)
        ends = count - 1
        head = lax.slice_in_dim(cells, 0, width, axis=dim)
        tail = lax.slice_in_dim(cells, cells.shape[dim] - width, cells.shape[dim], axis=dim)
        cells = jnp.concatenate(
            [
                lax.ppermute(tail, axis, [(i, (i + 1) % count) for i in range(ends)]),
                cells,
                lax.ppermute(head, axis, [((i + 1) % count, i) for i in range(ends)]),
            ],
            axis=dim,
        )
    return cells


def weight_matrix(tile_id, ping_ids, shift_ids, live_rows, tile_count):
    spacing = TILE_DEV * X // PING_DEV
    column = jnp.arange(ping_ids.shape[0] * 2 * C, dtype=jnp.int32)
    part_of = column // C % 2
    channel = column % C
    ping_cols = jnp.repeat(ping_ids, 2 * C)
    shift_cols = jnp.repeat(shift_ids, 2 * C)
    live_cols = jnp.repeat(live_rows, 2 * C)
    pixels = jnp.arange(X, dtype=jnp.int32)
    offset = tile_id * X - ping_cols * spacing - 2 * channel
    folded = jnp.remainder(pixels[:, None] + offset[None, :], phase_modulus)
    square = jnp.remainder(folded * folded, phase_modulus)
    phases = square.astype(jnp.float32) * (2.0 * math.pi / phase_modulus) + shift_cols.astype(
        jnp.float32
    )[None, :] * (math.pi / 4.0)
    scales = live_cols / jnp.sqrt(jnp.float32(C) * tile_count.astype(jnp.float32))
    cosine = jnp.cos(phases) * scales[None, :]
    sines = jnp.sin(phases) * scales[None, :]
    upper_rows = jnp.where(part_of[None, :] == 0, cosine, -sines)
    lower_rows = jnp.where(part_of[None, :] == 0, sines, cosine)
    return jnp.concatenate([upper_rows, lower_rows], axis=0).astype(jnp.bfloat16)


def focus_tile(received_data, received_labels):
    flat_rows = received_data.reshape((-1,) + received_data.shape[2:])
    flat_labels = received_labels.reshape(-1, 4)
    live_int = (flat_labels[:, 0] >= 0).astype(jnp.int32)
    ping_ids = flat_labels[:, 1]
    shift_ids = flat_labels[:, 2]
    tile_id = flat_labels[0, 3]
    tile_count = jnp.sum(live_int)
    block_len = flat_rows.shape[3]
    weights = weight_matrix(tile_id, ping_ids, shift_ids, live_int.astype(jnp.float32), tile_count)
    product = jnp.dot(weights, flat_rows.reshape(-1, block_len), preferred_element_type=jnp.float32)
    return product.reshape(2, X, block_len)


def focus(received):
    received_data, received_labels = received
    results = [focus_tile(received_data[:, 0], received_labels[:, 0])]
    return jnp.stack(results, axis=0)


def general_device(echoes, pairing, footprint, counts, offsets, earlier):
    ping_dev = echoes.shape[0]
    owners = lax.axis_size("ping")
    own_index = lax.axis_index("ping")
    channel_ids = jnp.arange(C, dtype=jnp.int32)
    front_pick = (pairing[:, 0, :, None] == channel_ids).astype(jnp.bfloat16)
    rear_pick = (pairing[:, 1, :, None] == channel_ids).astype(jnp.bfloat16)
    rear_rows = jnp.einsum("pkc,pzcr->pzkr", rear_pick, echoes, preferred_element_type=jnp.float32)
    inner_rows = jnp.einsum(
        "pkc,pzcr->pzkr", front_pick[1:], echoes[:-1], preferred_element_type=jnp.float32
    )
    last_ping = passed_along(echoes[-1], "ping", 1)
    lead_rows = jnp.einsum(
        "kc,zcr->zkr", front_pick[0], last_ping, preferred_element_type=jnp.float32
    )
    front_rows = jnp.concatenate([lead_rows[None], inner_rows], axis=0)
    cross_sum = jnp.sum(
        front_rows[:, 0] * rear_rows[:, 1] - front_rows[:, 1] * rear_rows[:, 0], axis=(1, 2)
    )
    front_energy = jnp.sum(front_rows * front_rows, axis=(1, 2, 3))
    rear_energy = jnp.sum(rear_rows * rear_rows, axis=(1, 2, 3))
    cross_sum, front_energy, rear_energy = lax.psum((cross_sum, front_energy, rear_energy), "rng")
    increment = cross_sum / (jnp.sqrt(front_energy * rear_energy) + small_value)
    running = jnp.cumsum(increment)
    before_turn = prefix(running[-1], "ping", jnp.add, jnp.float32(0.0))
    track_turn = before_turn + running
    cosine = jnp.cos(track_turn)[:, None, None]
    sines = jnp.sin(track_turn)[:, None, None]
    real_part = echoes[:, 0].astype(jnp.float32)
    imag_part = echoes[:, 1].astype(jnp.float32)
    corrected = jnp.stack(
        [real_part * cosine + imag_part * sines, imag_part * cosine - real_part * sines], axis=1
    ).astype(jnp.bfloat16)
    tile_total = footprint.shape[0]
    slot_cap = -(-MOST // owners)
    positions = jnp.arange(MOST, dtype=jnp.int32)
    in_list = positions[None, :] < counts[:, None]
    from_here = in_list & (footprint // ping_dev == own_index)
    order_here = jnp.cumsum(from_here.astype(jnp.int32), axis=1) - 1
    slot_ids = jnp.arange(slot_cap, dtype=jnp.int32)
    select = (from_here[:, None, :] & (order_here[:, None, :] == slot_ids[None, :, None])).astype(
        jnp.int32
    )
    place_ids = jnp.sum(select * (positions + 1)[None, None, :], axis=2) - 1
    local_ids = jnp.sum(select * (footprint % ping_dev)[:, None, :], axis=2)
    ping_ids = jnp.sum(select * footprint[:, None, :], axis=2)
    shift_ids = jnp.sum(select * offsets[:, None, :], axis=2)
    tile_ids = jnp.broadcast_to(jnp.arange(tile_total, dtype=jnp.int32)[:, None], place_ids.shape)
    labels = jnp.stack([place_ids, ping_ids, shift_ids, tile_ids], axis=2).reshape(
        owners, tile_total // owners, slot_cap, 4
    )
    block_len = corrected.shape[3]
    source = with_halo(corrected, (("rng", 3),), BAND)

    def cut_window(local_one, offset_one):
        return lax.dynamic_slice(
            source, (local_one, 0, 0, BAND + offset_one), (1, 2, C, block_len)
        )[0]

    outgoing = jax.vmap(cut_window)(local_ids.reshape(-1), shift_ids.reshape(-1))
    outgoing = outgoing.reshape((owners, tile_total // owners, slot_cap, 2, C, block_len))
    contribution = focus(
        (
            lax.all_to_all(outgoing, "ping", split_axis=0, concat_axis=0, tiled=True),
            lax.all_to_all(labels, "ping", split_axis=0, concat_axis=0, tiled=True),
        )
    )
    return (earlier.astype(jnp.float32) + contribution).astype(jnp.bfloat16)


LEAD = 4
VARIANTS = ((4, 4, 4), (4, 4, 4, 2), (4, 4, 4, 4, 4, 4))
LANES = 128
MIB = 1 << 20
SMEM = pl.BlockSpec(memory_space=pltpu.SMEM)
ANY = pl.BlockSpec(memory_space=pl.ANY)
COS_TERMS = (
    1.0, -19.73920440673828, 64.93911743164062, -85.45014190673828, 60.16762924194336,
    -25.967599868774414, 6.528658390045166,
)
SIN_TERMS = (
    6.2831854820251465, -41.34170150756836, 81.60513305664062, -76.70301818847656, 42.02592849731445,
    -14.899847030639648, 3.2381374835968018,
)


def bit_count(mask):
    mask = mask - ((mask >> 1) & 0x5555)
    mask = (mask & 0x3333) + ((mask >> 2) & 0x3333)
    mask = (mask + (mask >> 4)) & 0x0F0F
    return (mask + (mask >> 8)) & 0x1F


def each_bit(mask, place, visit):
    def body(_, carry):
        left, at = carry
        low = left & -left
        visit(at, bit_count(low - 1))
        return left ^ low, at + 1

    return lax.fori_loop(0, bit_count(mask), body, (mask, place))[1]


def link_list(masks, owners, s, axis, own, relay):
    chips = owners // 2
    near, other = (1, 4) if axis == 0 else (2, 2)
    base = owners * chips
    first = masks[base + axis * owners + s]
    direct = masks[s * chips + ((s >> 1) ^ near)] & ~first
    behind = s ^ other
    passed = masks[base + (1 - axis) * owners + behind]
    place = each_bit(first, jnp.int32(0), own)
    place = each_bit(direct, place, own)
    begin = jnp.maximum(place, 2 * LEAD)
    each_bit(passed, begin, lambda at, bit: relay(at, behind, bit, at - begin))


def plan_kernel(owners, ping_dev, cap, most, tiles, fp, cnt, me_ref, send, masks, total):
    chips = owners // 2
    shift = ping_dev.bit_length() - 1
    room = 4 * cap
    base = owners * chips
    me = me_ref[0]

    def clear(i, _):
        masks[i] = 0
        return 0

    lax.fori_loop(0, base, clear, 0)

    def clear_send(i, _):
        send[i] = 0
        return 0

    lax.fori_loop(0, 2 * room + 2 * cap, clear_send, 0)

    def one_tile(t, _):
        def entry(j, _):
            p = fp[t, j]
            at = (p >> shift) * chips + (t >> 1)
            masks[at] = masks[at] | lax.shift_left(jnp.int32(1), p & (ping_dev - 1))
            return 0

        return lax.fori_loop(0, cnt[t], entry, 0)

    lax.fori_loop(0, tiles, one_tile, 0)

    def split(s, _):
        chip = s >> 1
        far = masks[s * chips + (chip ^ 3)]
        n = bit_count(far)
        over_y = bit_count(masks[(s ^ 2) * chips + (chip ^ 3)])
        over_x = bit_count(masks[(s ^ 4) * chips + (chip ^ 3)])
        want = (n + over_x - over_y + 1) >> 1
        want = jnp.minimum(jnp.maximum(want, jnp.maximum(n - cap, 0)), jnp.minimum(n, cap))

        def take(_, carry):
            left, taken = carry
            low = left & -left
            return left ^ low, taken | low

        left, taken = lax.fori_loop(0, want, take, (far, jnp.int32(0)))
        masks[base + s] = taken
        masks[base + owners + s] = left
        return 0

    lax.fori_loop(0, owners, split, 0)

    def longest(s, most_yet):
        for axis, near, other in ((0, 1, 4), (1, 2, 2)):
            own = bit_count(masks[base + axis * owners + s] | masks[s * chips + ((s >> 1) ^ near)])
            passed = bit_count(masks[base + (1 - axis) * owners + (s ^ other)])
            length = jnp.where(passed > 0, jnp.maximum(own, 2 * LEAD) + passed, own)
            most_yet = jnp.maximum(most_yet, length)
        return most_yet

    total[0] = lax.fori_loop(0, owners, longest, jnp.int32(0))

    for axis in range(2):

        def own(at, bit, axis=axis):
            send[axis * room + at] = bit

        def relay(at, behind, bit, i, axis=axis):
            send[axis * room + at] = ping_dev + i

        link_list(masks, owners, me, axis, own, relay)

    for k, tile in ((0, me), (1, me ^ 1)):

        def mine(j, at, k=k, tile=tile):
            p = fp[tile, j]
            here = (p >> shift) == me

            @pl.when(here)
            def _():
                send[2 * room + k * cap + at] = p & (ping_dev - 1)

            return at + here.astype(jnp.int32)

        lax.fori_loop(0, cnt[tile], mine, jnp.int32(0))


def places_kernel(owners, ping_dev, cap, fp, cnt, off, masks, me_ref, table, back):
    shift = ping_dev.bit_length() - 1
    room = 4 * cap
    count = 4 * room + 2 * cap
    me = me_ref[0]

    def clear(i, _):
        table[i] = 0
        return 0

    lax.fori_loop(0, 3 * count, clear, 0)

    def clear_back(i, _):
        back[i] = 0
        return 0

    lax.fori_loop(0, owners * ping_dev, clear_back, 0)

    def note(j, _):
        back[fp[me, j]] = j + 1
        return 0

    lax.fori_loop(0, cnt[me], note, 0)

    def put(at, ping):
        j = back[ping]
        table[at] = ping
        table[count + at] = off[me, jnp.maximum(j - 1, 0)]
        table[2 * count + at] = (j > 0).astype(jnp.int32)

    for a, (axis, flip) in enumerate(((0, 2), (1, 4), (0, 3), (1, 5))):
        s = me ^ flip

        def own(at, bit, a=a, s=s):
            put(a * room + at, s * ping_dev + bit)

        def relay(at, behind, bit, i, a=a):
            put(a * room + at, behind * ping_dev + bit)

        link_list(masks, owners, s, axis, own, relay)

    for k, s in ((0, me), (1, me ^ 1)):

        def listed(j, at, k=k, s=s):
            p = fp[me, j]
            here = (p >> shift) == s

            @pl.when(here)
            def _():
                put(4 * room + k * cap + at, p)

            return at + here.astype(jnp.int32)

        lax.fori_loop(0, cnt[me], listed, jnp.int32(0))


def gather_kernel(ping_dev, cap, span, local, relayed, send, echoes, halo, *refs):
    room = 4 * cap
    begin, n = span
    sources = refs[: 2 * relayed]
    outs = refs[2 * relayed : -1]
    sems = refs[-1]
    width = echoes.shape[2]
    jobs = []
    for axis in range(2):
        for i in range(n):
            jobs.append((axis * room + begin + i, outs[axis], i, axis))
    if local:
        for k in range(2):
            for i in range(cap):
                jobs.append((2 * room + k * cap + i, outs[2 + k], i, None))

    def copies(job, number):
        at, out, i, axis = job
        index = send[at]
        here = jnp.minimum(index, ping_dev - 1)
        groups = [
            (
                index < ping_dev,
                [
                    pltpu.make_async_copy(
                        echoes.at[here], out.at[i, :, pl.ds(0, width)], sems.at[number, 0]
                    ),
                    pltpu.make_async_copy(
                        halo.at[here], out.at[i, :, pl.ds(width, LANES)], sems.at[number, 1]
                    ),
                ],
            )
        ]
        if axis is not None:
            for k in range(relayed):
                low = ping_dev + k * LEAD
                chosen = (index >= low) & (index < low + LEAD)
                source = sources[2 * k + 1 - axis]
                from_place = jnp.clip(index - low, 0, LEAD - 1)
                groups.append(
                    (chosen, [pltpu.make_async_copy(source.at[from_place], out.at[i], sems.at[number, 0])])
                )
        return groups

    for number, job in enumerate(jobs):
        for chosen, group in copies(job, number):

            @pl.when(chosen)
            def _(group=group):
                for copy in group:
                    copy.start()

    for number, job in enumerate(jobs):
        for chosen, group in copies(job, number):

            @pl.when(chosen)
            def _(group=group):
                for copy in group:
                    copy.wait()


def weights_kernel(ping_dev, spacing, pixels, table, where, cnt, me_ref, out):
    count = table.shape[0] // 3
    me = me_ref[0]
    step = pl.program_id(0)
    lane = lax.broadcasted_iota(jnp.int32, (1, LANES), 1)
    second = lane >= 2 * C
    part = (lane // C) % 2
    channel = lane % C
    bases, shifts, lives = [], [], []
    for k in range(2):
        at = where[2 * step + k]
        d = me * pixels - table[at] * spacing
        bases.append(jnp.full((1, LANES), d, jnp.int32))
        shifts.append(jnp.full((1, LANES), table[count + at], jnp.int32))
        lives.append(jnp.full((1, LANES), table[2 * count + at], jnp.int32))
    pick = lambda pair: jnp.where(second, pair[1], pair[0])
    base = jnp.remainder(pick(bases) - 2 * channel, phase_modulus).astype(jnp.float32)
    turn = pick(shifts).astype(jnp.float32) * 0.125 + part.astype(jnp.float32) * 0.25
    amount = jnp.full((1, LANES), cnt[me], jnp.int32).astype(jnp.float32)
    scale = pick(lives).astype(jnp.float32) / jnp.sqrt(jnp.float32(C) * amount)
    modulus = jnp.float32(phase_modulus)
    inverse = jnp.float32(1.0 / phase_modulus)
    strip = 64
    rows = lax.broadcasted_iota(jnp.int32, (strip, LANES), 0).astype(jnp.float32)

    def one_strip(r, _):
        start = pl.multiple_of(r * strip, strip)
        m = (rows + start.astype(jnp.float32)) + base
        m = jnp.where(m > 0.5 * phase_modulus, m - modulus, m)
        square = m * m
        rest = square - jnp.floor(square * inverse + 0.5) * modulus
        g = rest * inverse + turn
        g = g - jnp.floor(g + 0.5)
        u = g * g
        cosine = jnp.float32(COS_TERMS[-1])
        for term in COS_TERMS[-2::-1]:
            cosine = cosine * u + term
        sine = jnp.float32(SIN_TERMS[-1])
        for term in SIN_TERMS[-2::-1]:
            sine = sine * u + term
        out[pl.ds(start, strip), :] = (cosine * scale).astype(out.dtype)
        out[pl.ds(pl.multiple_of(pixels + start, strip), strip), :] = (sine * g * scale).astype(out.dtype)
        return 0

    lax.fori_loop(0, pixels // strip, one_strip, 0)


def focus_kernel(slots, sizes, table, where, turn, weights, *refs):
    arrays = refs[: len(sizes)]
    total, out, window = refs[len(sizes) :]
    count = table.shape[0] // 3
    width = window.shape[1]
    blocks = width // LANES
    rows = 16
    column = total.shape[1]

    @pl.when(pl.program_id(0) == 0)
    def _():
        lane = lax.broadcasted_iota(jnp.int32, (rows, LANES), 1)
        first = 0
        for array, size in zip(arrays, sizes):

            def one_slot(i, _, array=array, first=first):
                slot = first + i
                at = where[slot]
                ping = table[at]
                offset = table[count + at]
                cosine = turn[0, ping]
                sine = turn[1, ping]
                roll = (LANES - offset) & (LANES - 1)

                def strip(r, _, forward):
                    top = pl.multiple_of(r * rows, rows)
                    place = pl.multiple_of(slot * 2 * C + r * rows, rows)

                    def rolled(b):
                        cut = pl.ds((b % (blocks + 1)) * LANES, LANES)
                        real = array[i, pl.ds(top, rows), cut].astype(jnp.float32)
                        imag = array[i, pl.ds(pl.multiple_of(C + top, rows), rows), cut].astype(jnp.float32)
                        return (
                            pltpu.roll(real * cosine + imag * sine, roll, 1),
                            pltpu.roll(imag * cosine - real * sine, roll, 1),
                        )

                    keep = lane < LANES - offset if forward else lane >= -offset
                    before = rolled(0 if forward else -1)
                    for b in range(blocks):
                        after = rolled(b + 1 if forward else b)
                        now, beside = (before, after) if forward else (after, before)
                        cut = pl.ds(b * LANES, LANES)
                        window[pl.ds(place, rows), cut] = jnp.where(keep, now[0], beside[0]).astype(window.dtype)
                        window[pl.ds(pl.multiple_of(place + C, rows), rows), cut] = jnp.where(
                            keep, now[1], beside[1]
                        ).astype(window.dtype)
                        before = after
                    return 0

                @pl.when(offset >= 0)
                def _():
                    lax.fori_loop(0, C // rows, functools.partial(strip, forward=True), 0)

                @pl.when(offset < 0)
                def _():
                    lax.fori_loop(0, C // rows, functools.partial(strip, forward=False), 0)

                return 0

            lax.fori_loop(0, size, one_slot, 0)
            first += size

    tall = total.shape[0]
    piece = min(tall, 512)
    here = pl.ds(pl.multiple_of(pl.program_id(0) * column, column), column)

    def one_piece(r, _):
        part = pl.ds(pl.multiple_of(r * piece, piece), piece)
        product = jnp.dot(weights[part, :], window[:, here], preferred_element_type=jnp.float32)
        out[part, :] = (total[part, :].astype(jnp.float32) + product).astype(out.dtype)
        return 0

    lax.fori_loop(0, tall // piece, one_piece, 0)


def params(mib):
    return pltpu.CompilerParams(vmem_limit_bytes=mib * MIB)


def swap(shard, by):
    return lax.ppermute(shard, "ping", [(i, i ^ by) for i in range(lax.axis_size("ping"))])


def turns(echoes, pairing):
    owners, ranges = lax.axis_size("ping"), lax.axis_size("rng")
    channel_ids = jnp.arange(C, dtype=jnp.int32)
    front_pick = (pairing[:, 0, :, None] == channel_ids).astype(jnp.bfloat16)
    rear_pick = (pairing[:, 1, :, None] == channel_ids).astype(jnp.bfloat16)
    last_ping = passed_along(echoes[-1], "ping", 1)
    rear_rows = jnp.einsum("pkc,pzcr->pzkr", rear_pick, echoes, preferred_element_type=jnp.float32)
    inner_rows = jnp.einsum(
        "pkc,pzcr->pzkr", front_pick[1:], echoes[:-1], preferred_element_type=jnp.float32
    )
    lead_rows = jnp.einsum(
        "kc,zcr->zkr", front_pick[0], last_ping, preferred_element_type=jnp.float32
    )
    front_rows = jnp.concatenate([lead_rows[None], inner_rows], axis=0)
    cross_sum = jnp.sum(
        front_rows[:, 0] * rear_rows[:, 1] - front_rows[:, 1] * rear_rows[:, 0], axis=(1, 2)
    )
    front_energy = jnp.sum(front_rows * front_rows, axis=(1, 2, 3))
    rear_energy = jnp.sum(rear_rows * rear_rows, axis=(1, 2, 3))
    parts = jnp.stack([cross_sum, front_energy, rear_energy])
    every = lax.all_gather(parts, ("ping", "rng"))
    sums = jnp.sum(every.reshape(owners, ranges, 3, -1), axis=1)
    cross_sum, front_energy, rear_energy = [sums[:, i].reshape(-1) for i in range(3)]
    increment = cross_sum / (jnp.sqrt(front_energy * rear_energy) + small_value)
    order = jnp.arange(increment.shape[0], dtype=jnp.int32)
    track_turn = jnp.sum(jnp.where(order[None, :] <= order[:, None], increment[None, :], 0.0), axis=1)
    return jnp.stack([jnp.cos(track_turn), jnp.sin(track_turn)])


def chunked(chunks, echoes, pairing, counts, me, flat, halo, send, table, earlier):
    owners = lax.axis_size("ping")
    ping_dev, channels, width = flat.shape
    cap = -(-MOST // owners)
    room = 4 * cap
    wide = width + LANES
    pixels = earlier.shape[2]
    spacing = pixels * earlier.shape[0] // ping_dev
    slot = lambda n: jax.ShapeDtypeStruct((n, channels, wide), flat.dtype)
    received, groups = [], []
    begin = 0
    local = None
    for c, n in enumerate(chunks):
        relayed = min(max(c - 1, 0), 2)
        shapes = [slot(n), slot(n)] + ([slot(cap), slot(cap)] if c == 0 else [])
        moved = pl.pallas_call(
            functools.partial(gather_kernel, ping_dev, cap, (begin, n), c == 0, relayed),
            out_shape=shapes,
            in_specs=[SMEM] + [ANY] * (2 + 2 * relayed),
            out_specs=[ANY] * len(shapes),
            scratch_shapes=[pltpu.SemaphoreType.DMA((2 * n + (2 * cap if c == 0 else 0), 2))],
            cost_estimate=pl.CostEstimate(flops=0, bytes_accessed=4 * n * channels * wide * 2, transcendentals=0),
            name="gather",
        )(send, flat, halo, *[a for pair in received[:relayed] for a in pair])
        over_x, over_y = swap(moved[0], 2), swap(moved[1], 4)
        received.append((over_x, over_y))
        arrays = [over_x, over_y, swap(over_x, 1), swap(over_y, 1)]
        places = [a * room + begin + i for a in range(4) for i in range(n)]
        if c == 0:
            arrays = [moved[2], swap(moved[3], 1)] + arrays
            places = [4 * room + i for i in range(2 * cap)] + places
        groups.append((arrays, places))
        begin += n

    weights = []
    for arrays, places in groups:
        slots = len(places)
        weights.append(
            pl.pallas_call(
                functools.partial(weights_kernel, ping_dev, spacing, pixels),
                grid=(slots // 2,),
                in_specs=[SMEM] * 4,
                out_specs=pl.BlockSpec((2 * pixels, LANES), lambda i: (0, i)),
                out_shape=jax.ShapeDtypeStruct((2 * pixels, slots * 2 * C), jnp.bfloat16),
                cost_estimate=pl.CostEstimate(
                    flops=40 * pixels * slots * 2 * C, bytes_accessed=2 * pixels * slots * 4 * C, transcendentals=0
                ),
                name="weights",
            )(table, np.asarray(places, np.int32), counts, me)
        )

    turn = turns(echoes, pairing)
    total = earlier.reshape(2 * pixels, width)
    column = 256
    for number, ((arrays, places), weight) in enumerate(zip(groups, weights)):
        slots = len(places)
        deep = slots * 2 * C
        final = number == len(groups) - 1
        sizes = [a.shape[0] for a in arrays]
        kind = jnp.bfloat16 if final else jnp.float32
        total = pl.pallas_call(
            functools.partial(focus_kernel, slots, sizes),
            grid=(width // column,),
            in_specs=[SMEM, SMEM, SMEM]
            + [pl.BlockSpec(memory_space=pltpu.VMEM)] * (1 + len(arrays))
            + [pl.BlockSpec((2 * pixels, column), lambda i: (0, i))],
            out_specs=pl.BlockSpec((2 * pixels, column), lambda i: (0, i)),
            out_shape=jax.ShapeDtypeStruct((2 * pixels, width), kind),
            scratch_shapes=[pltpu.VMEM((deep, width), jnp.bfloat16)],
            compiler_params=params(48),
            cost_estimate=pl.CostEstimate(
                flops=2 * 2 * pixels * deep * width,
                bytes_accessed=2 * pixels * width * 8 + deep * (width + 2 * pixels) * 2,
                transcendentals=0,
            ),
            name="focus",
        )(table, np.asarray(places, np.int32), turn, weight, *arrays, total)
    return total.reshape(earlier.shape)


def paired_device(echoes, pairing, footprint, counts, offsets, earlier):
    owners, ranges = lax.axis_size("ping"), lax.axis_size("rng")
    tiles = footprint.shape[0]
    ping_dev, _, _, width = echoes.shape
    cap = -(-MOST // owners)
    room = 4 * cap
    base = owners * (owners // 2)
    count = 4 * room + 2 * cap
    flat = echoes.reshape(ping_dev, 2 * C, width)
    head = lax.slice_in_dim(flat, 0, LANES, axis=2)
    tail = lax.slice_in_dim(flat, width - LANES, width, axis=2)
    after = lax.ppermute(head, "rng", [(i + 1, i) for i in range(ranges - 1)])
    ahead = lax.ppermute(tail, "rng", [(i, i + 1) for i in range(ranges - 1)])
    halo = jnp.where(jnp.arange(LANES) < BAND, after, ahead)
    me = lax.axis_index("ping").astype(jnp.int32).reshape(1)
    whole = lambda *shape: jax.ShapeDtypeStruct(shape, jnp.int32)
    send, masks, total = pl.pallas_call(
        functools.partial(plan_kernel, owners, ping_dev, cap, MOST, tiles),
        out_shape=[whole(2 * room + 2 * cap), whole(base + 2 * owners), whole(1)],
        in_specs=[SMEM] * 3,
        out_specs=[SMEM] * 3,
        name="plan",
    )(footprint, counts, me)
    table = pl.pallas_call(
        functools.partial(places_kernel, owners, ping_dev, cap),
        out_shape=whole(3 * count),
        in_specs=[SMEM] * 5,
        out_specs=SMEM,
        scratch_shapes=[pltpu.SMEM((owners * ping_dev,), jnp.int32)],
        name="places",
    )(footprint, counts, offsets, masks, me)
    lengths = np.asarray([sum(v) for v in VARIANTS[:-1]], np.int32)
    chosen = jnp.sum((total > lengths).astype(jnp.int32))
    return lax.switch(
        chosen,
        [functools.partial(chunked, v) for v in VARIANTS],
        echoes, pairing, counts, me, flat, halo, send, table, earlier,
    )


def per_device(echoes, pairing, footprint, counts, offsets, earlier):
    owners = lax.axis_size("ping")
    ping_dev = echoes.shape[0]
    paired = (
        owners == 8
        and footprint.shape[0] == owners
        and ping_dev <= 16
        and ping_dev & (ping_dev - 1) == 0
        and sum(VARIANTS[-1]) >= 4 * -(-MOST // owners)
    )
    device = paired_device if paired else general_device
    return device(echoes, pairing, footprint, counts, offsets, earlier)


def solution(mesh):
    return jax.shard_map(
        per_device,
        mesh=mesh,
        in_specs=(
            P("ping", None, None, "rng"),
            P("ping", None, None),
            P(),
            P(),
            P(),
            P("ping", None, None, "rng"),
        ),
        out_specs=P("ping", None, None, "rng"),
        check_vma=False,
    )
```

```python
import functools
import math

import jax
import jax.numpy as jnp
import numpy as np
from jax import lax
from jax.experimental import pallas as pl
from jax.experimental.pallas import tpu as pltpu
from jax.sharding import PartitionSpec as P

C = 32
X = 1024
BAND = 64
MOST = 48
TILE_DEV = 1
PING_DEV = 16


phase_modulus = 4099
small_value = 1e-06


def passed_along(shard, axis, by):
    length = lax.axis_size(axis)
    pairs = [(i, i + by) for i in range(length) if 0 <= i + by < length]
    return lax.ppermute(shard, axis, pairs)


def prefix(shard, axis, combine, identity):
    length, position = (lax.axis_size(axis), lax.axis_index(axis))
    everything = lax.all_gather(shard, axis)
    start = jnp.broadcast_to(jnp.asarray(identity, shard.dtype), shard.shape)

    def step(k, before):
        reached = k < position
        new = combine(before, everything[k])
        return jnp.where(reached, new, before)

    return lax.fori_loop(0, length, step, start)


def with_halo(cells, sides, width):
    for axis, dim in sides:
        count = lax.axis_size(axis)
        ends = count - 1
        head = lax.slice_in_dim(cells, 0, width, axis=dim)
        tail = lax.slice_in_dim(cells, cells.shape[dim] - width, cells.shape[dim], axis=dim)
        cells = jnp.concatenate(
            [
                lax.ppermute(tail, axis, [(i, (i + 1) % count) for i in range(ends)]),
                cells,
                lax.ppermute(head, axis, [((i + 1) % count, i) for i in range(ends)]),
            ],
            axis=dim,
        )
    return cells


def weight_matrix(tile_id, ping_ids, shift_ids, live_rows, tile_count):
    spacing = TILE_DEV * X // PING_DEV
    column = jnp.arange(ping_ids.shape[0] * 2 * C, dtype=jnp.int32)
    part_of = column // C % 2
    channel = column % C
    ping_cols = jnp.repeat(ping_ids, 2 * C)
    shift_cols = jnp.repeat(shift_ids, 2 * C)
    live_cols = jnp.repeat(live_rows, 2 * C)
    pixels = jnp.arange(X, dtype=jnp.int32)
    offset = tile_id * X - ping_cols * spacing - 2 * channel
    folded = jnp.remainder(pixels[:, None] + offset[None, :], phase_modulus)
    square = jnp.remainder(folded * folded, phase_modulus)
    phases = square.astype(jnp.float32) * (2.0 * math.pi / phase_modulus) + shift_cols.astype(
        jnp.float32
    )[None, :] * (math.pi / 4.0)
    scales = live_cols / jnp.sqrt(jnp.float32(C) * tile_count.astype(jnp.float32))
    cosine = jnp.cos(phases) * scales[None, :]
    sines = jnp.sin(phases) * scales[None, :]
    upper_rows = jnp.where(part_of[None, :] == 0, cosine, -sines)
    lower_rows = jnp.where(part_of[None, :] == 0, sines, cosine)
    return jnp.concatenate([upper_rows, lower_rows], axis=0).astype(jnp.bfloat16)


def focus_tile(received_data, received_labels):
    flat_rows = received_data.reshape((-1,) + received_data.shape[2:])
    flat_labels = received_labels.reshape(-1, 4)
    live_int = (flat_labels[:, 0] >= 0).astype(jnp.int32)
    ping_ids = flat_labels[:, 1]
    shift_ids = flat_labels[:, 2]
    tile_id = flat_labels[0, 3]
    tile_count = jnp.sum(live_int)
    block_len = flat_rows.shape[3]
    weights = weight_matrix(tile_id, ping_ids, shift_ids, live_int.astype(jnp.float32), tile_count)
    product = jnp.dot(weights, flat_rows.reshape(-1, block_len), preferred_element_type=jnp.float32)
    return product.reshape(2, X, block_len)


def focus(received):
    received_data, received_labels = received
    results = [focus_tile(received_data[:, 0], received_labels[:, 0])]
    return jnp.stack(results, axis=0)


def general_device(echoes, pairing, footprint, counts, offsets, earlier):
    ping_dev = echoes.shape[0]
    owners = lax.axis_size("ping")
    own_index = lax.axis_index("ping")
    channel_ids = jnp.arange(C, dtype=jnp.int32)
    front_pick = (pairing[:, 0, :, None] == channel_ids).astype(jnp.bfloat16)
    rear_pick = (pairing[:, 1, :, None] == channel_ids).astype(jnp.bfloat16)
    rear_rows = jnp.einsum("pkc,pzcr->pzkr", rear_pick, echoes, preferred_element_type=jnp.float32)
    inner_rows = jnp.einsum(
        "pkc,pzcr->pzkr", front_pick[1:], echoes[:-1], preferred_element_type=jnp.float32
    )
    last_ping = passed_along(echoes[-1], "ping", 1)
    lead_rows = jnp.einsum(
        "kc,zcr->zkr", front_pick[0], last_ping, preferred_element_type=jnp.float32
    )
    front_rows = jnp.concatenate([lead_rows[None], inner_rows], axis=0)
    cross_sum = jnp.sum(
        front_rows[:, 0] * rear_rows[:, 1] - front_rows[:, 1] * rear_rows[:, 0], axis=(1, 2)
    )
    front_energy = jnp.sum(front_rows * front_rows, axis=(1, 2, 3))
    rear_energy = jnp.sum(rear_rows * rear_rows, axis=(1, 2, 3))
    cross_sum, front_energy, rear_energy = lax.psum((cross_sum, front_energy, rear_energy), "rng")
    increment = cross_sum / (jnp.sqrt(front_energy * rear_energy) + small_value)
    running = jnp.cumsum(increment)
    before_turn = prefix(running[-1], "ping", jnp.add, jnp.float32(0.0))
    track_turn = before_turn + running
    cosine = jnp.cos(track_turn)[:, None, None]
    sines = jnp.sin(track_turn)[:, None, None]
    real_part = echoes[:, 0].astype(jnp.float32)
    imag_part = echoes[:, 1].astype(jnp.float32)
    corrected = jnp.stack(
        [real_part * cosine + imag_part * sines, imag_part * cosine - real_part * sines], axis=1
    ).astype(jnp.bfloat16)
    tile_total = footprint.shape[0]
    slot_cap = -(-MOST // owners)
    positions = jnp.arange(MOST, dtype=jnp.int32)
    in_list = positions[None, :] < counts[:, None]
    from_here = in_list & (footprint // ping_dev == own_index)
    order_here = jnp.cumsum(from_here.astype(jnp.int32), axis=1) - 1
    slot_ids = jnp.arange(slot_cap, dtype=jnp.int32)
    select = (from_here[:, None, :] & (order_here[:, None, :] == slot_ids[None, :, None])).astype(
        jnp.int32
    )
    place_ids = jnp.sum(select * (positions + 1)[None, None, :], axis=2) - 1
    local_ids = jnp.sum(select * (footprint % ping_dev)[:, None, :], axis=2)
    ping_ids = jnp.sum(select * footprint[:, None, :], axis=2)
    shift_ids = jnp.sum(select * offsets[:, None, :], axis=2)
    tile_ids = jnp.broadcast_to(jnp.arange(tile_total, dtype=jnp.int32)[:, None], place_ids.shape)
    labels = jnp.stack([place_ids, ping_ids, shift_ids, tile_ids], axis=2).reshape(
        owners, tile_total // owners, slot_cap, 4
    )
    block_len = corrected.shape[3]
    source = with_halo(corrected, (("rng", 3),), BAND)

    def cut_window(local_one, offset_one):
        return lax.dynamic_slice(
            source, (local_one, 0, 0, BAND + offset_one), (1, 2, C, block_len)
        )[0]

    outgoing = jax.vmap(cut_window)(local_ids.reshape(-1), shift_ids.reshape(-1))
    outgoing = outgoing.reshape((owners, tile_total // owners, slot_cap, 2, C, block_len))
    contribution = focus(
        (
            lax.all_to_all(outgoing, "ping", split_axis=0, concat_axis=0, tiled=True),
            lax.all_to_all(labels, "ping", split_axis=0, concat_axis=0, tiled=True),
        )
    )
    return (earlier.astype(jnp.float32) + contribution).astype(jnp.bfloat16)


LEAD = 4
VARIANTS = ((4, 4, 4), (4, 4, 4, 2), (4, 4, 4, 4, 4, 4))
LANES = 128
SMALL = pl.CostEstimate(flops=1024, bytes_accessed=1024, transcendentals=0)
MIB = 1 << 20
COLUMN = 512
PIECE = 1024
FOCUS_MIB = 40
SMEM = pl.BlockSpec(memory_space=pltpu.SMEM)
ANY = pl.BlockSpec(memory_space=pl.ANY)
VMEM = pl.BlockSpec(memory_space=pltpu.VMEM)
COS_TERMS = (
    1.0, -19.73920440673828, 64.93911743164062, -85.45014190673828, 60.16762924194336,
    -25.967599868774414, 6.528658390045166,
)
SIN_TERMS = (
    6.2831854820251465, -41.34170150756836, 81.60513305664062, -76.70301818847656, 42.02592849731445,
    -14.899847030639648, 3.2381374835968018,
)


def bit_count(mask):
    down = lax.shift_right_logical
    mask = mask - (down(mask, 1) & 0x55555555)
    mask = (mask & 0x33333333) + (down(mask, 2) & 0x33333333)
    mask = (mask + down(mask, 4)) & 0x0F0F0F0F
    mask = mask + down(mask, 8)
    return (mask + down(mask, 16)) & 0x3F


def each_bit(mask, place, visit):
    def body(_, carry):
        left, at = carry
        low = left & -left
        visit(at, bit_count(low - 1))
        return left ^ low, at + 1

    return lax.fori_loop(0, bit_count(mask), body, (mask, place))[1]


def link_list(masks, owners, s, axis, own, relay):
    chips = owners // 2
    near, other = (1, 4) if axis == 0 else (2, 2)
    base = owners * chips
    chip = s >> 1
    behind = s ^ other
    place = each_bit(masks[base + axis * owners + s], jnp.int32(0), lambda at, bit: own(at, chip ^ 3, bit))
    place = each_bit(masks[s * chips + (chip ^ near)], place, lambda at, bit: own(at, chip ^ near, bit))
    begin = jnp.maximum(place, 2 * LEAD)
    passed = masks[base + (1 - axis) * owners + behind]
    each_bit(passed, begin, lambda at, bit: relay(at, behind, chip ^ near, bit, at - begin))


def plan_kernel(owners, ping_dev, cap, tiles, fp, cnt, off, me_ref, send, masks, shifts, total):
    chips = owners // 2
    bits = ping_dev.bit_length() - 1
    room = 4 * cap
    base = owners * chips
    pings = owners * ping_dev
    places = 2 * room + 2 * cap
    me = me_ref[0]

    def clear(i, _):
        masks[i] = 0
        return 0

    lax.fori_loop(0, base, clear, 0, unroll=8)

    def clear_send(i, _):
        send[i] = 0
        return 0

    lax.fori_loop(0, 2 * places, clear_send, 0, unroll=12)

    def one_tile(t, _):
        def entry(j, _):
            p = fp[t, j]
            at = (p >> bits) * chips + (t >> 1)
            masks[at] = masks[at] | lax.shift_left(jnp.int32(1), (p & (ping_dev - 1)) + (t & 1) * ping_dev)
            shifts[t * pings + p] = off[t, j]
            return 0

        return lax.fori_loop(0, cnt[t], entry, 0)

    lax.fori_loop(0, tiles, one_tile, 0)

    def split(s, _):
        chip = s >> 1
        far = masks[s * chips + (chip ^ 3)]
        n = bit_count(far)
        over_y = bit_count(masks[(s ^ 2) * chips + (chip ^ 3)])
        over_x = bit_count(masks[(s ^ 4) * chips + (chip ^ 3)])
        want = (n + over_x - over_y + 1) >> 1
        want = jnp.minimum(jnp.maximum(want, jnp.maximum(n - cap, 0)), jnp.minimum(n, cap))

        def take(_, carry):
            left, taken = carry
            low = left & -left
            return left ^ low, taken | low

        left, taken = lax.fori_loop(0, want, take, (far, jnp.int32(0)))
        masks[base + s] = taken
        masks[base + owners + s] = left
        return 0

    lax.fori_loop(0, owners, split, 0)

    def longest(s, most_yet):
        for axis, near, other in ((0, 1, 4), (1, 2, 2)):
            own = bit_count(masks[base + axis * owners + s]) + bit_count(masks[s * chips + ((s >> 1) ^ near)])
            passed = bit_count(masks[base + (1 - axis) * owners + (s ^ other)])
            length = jnp.where(passed > 0, jnp.maximum(own, 2 * LEAD) + passed, own)
            most_yet = jnp.maximum(most_yet, length)
        return most_yet

    length = lax.fori_loop(0, owners, longest, jnp.int32(0))
    chosen = jnp.int32(0)
    for variant in VARIANTS[:-1]:
        chosen = chosen + (length > sum(variant)).astype(jnp.int32)
    total[0] = chosen

    for axis in range(2):

        def own(at, chip, bit, axis=axis):
            ping = bit & (ping_dev - 1)
            tile = 2 * chip + (bit >> bits)
            send[axis * room + at] = ping
            send[places + axis * room + at] = shifts[tile * pings + me * ping_dev + ping]

        def relay(at, behind, chip, bit, i, axis=axis):
            send[axis * room + at] = ping_dev + i

        link_list(masks, owners, me, axis, own, relay)

    for k, tile in ((0, me), (1, me ^ 1)):

        def mine(j, at, k=k, tile=tile):
            p = fp[tile, j]
            here = (p >> bits) == me

            @pl.when(here)
            def _():
                send[2 * room + k * cap + at] = p & (ping_dev - 1)
                send[places + 2 * room + k * cap + at] = off[tile, j]

            return at + here.astype(jnp.int32)

        lax.fori_loop(0, cnt[tile], mine, jnp.int32(0))


def places_kernel(owners, ping_dev, cap, fp, cnt, off, masks, shifts, me_ref, table):
    bits = ping_dev.bit_length() - 1
    room = 4 * cap
    count = 4 * room + 2 * cap
    pings = owners * ping_dev
    me = me_ref[0]

    def clear(i, _):
        table[i] = 0
        return 0

    lax.fori_loop(0, 3 * count, clear, 0, unroll=12)

    def put(at, tile, ping):
        @pl.when(tile == me)
        def _():
            table[at] = ping
            table[count + at] = shifts[tile * pings + ping]
            table[2 * count + at] = 1

    for a, (axis, flip) in enumerate(((0, 2), (1, 4), (0, 3), (1, 5))):
        s = me ^ flip

        def own(at, chip, bit, a=a, s=s):
            put(a * room + at, 2 * chip + (bit >> bits), s * ping_dev + (bit & (ping_dev - 1)))

        def relay(at, behind, chip, bit, i, a=a):
            put(a * room + at, 2 * chip + (bit >> bits), behind * ping_dev + (bit & (ping_dev - 1)))

        link_list(masks, owners, s, axis, own, relay)

    for k, s in ((0, me), (1, me ^ 1)):

        def listed(j, at, k=k, s=s):
            p = fp[me, j]
            here = (p >> bits) == s

            @pl.when(here)
            def _():
                put(4 * room + k * cap + at, me, p)

            return at + here.astype(jnp.int32)

        lax.fori_loop(0, cnt[me], listed, jnp.int32(0))


def gather_kernel(ping_dev, places, spans, send, echoes, halo, *refs):
    outs, stage, sems = refs[-len(spans) - 2 : -2], refs[-2], refs[-1]
    sources = refs[: -len(spans) - 2]
    width = echoes.shape[2]
    blocks = width // LANES
    lane = lax.broadcasted_iota(jnp.int32, (2 * C, LANES), 1)
    jobs = [(begin + i, out, i, axis) for (begin, n, axis), out in zip(spans, outs) for i in range(n)]

    def copies(number):
        at, out, i, axis = jobs[number]
        index = send[at]
        here = jnp.minimum(index, ping_dev - 1)
        plain = [
            pltpu.make_async_copy(echoes.at[here], stage.at[number, :, pl.ds(0, width)], sems.at[number, 0]),
            pltpu.make_async_copy(halo.at[here], stage.at[number, :, pl.ds(width, LANES)], sems.at[number, 1]),
        ]
        if not sources:
            return [(None, plain)]
        groups = [(index < ping_dev, plain)]
        for k in range(len(sources) // 2):
            low = ping_dev + k * LEAD
            chosen = (index >= low) & (index < low + LEAD)
            source = sources[2 * k + 1 - axis].at[jnp.clip(index - low, 0, LEAD - 1)]
            groups.append((chosen, [pltpu.make_async_copy(source, out.at[i], sems.at[number, 0])]))
        return groups

    def act_on(number, act):
        for chosen, group in copies(number):
            if chosen is None:
                for copy in group:
                    act(copy)
            else:

                @pl.when(chosen)
                def _(group=group):
                    for copy in group:
                        act(copy)

    for number in range(len(jobs)):
        act_on(number, lambda copy: copy.start())
    for number in range(len(jobs)):
        act_on(number, lambda copy: copy.wait())

    number = 0
    for (begin, n, _), out in zip(spans, outs):

        def cut(i, _, begin=begin, out=out, number=number):
            offset = send[places + begin + i]
            within = offset & (LANES - 1)
            roll = (LANES - within) & (LANES - 1)
            keep = lane < LANES - within
            low = jnp.where(offset < 0, -LANES, 0)

            def rolled(b):
                start = low + b * LANES
                if b == 0:
                    start = jnp.where(start < 0, width, start)
                span = pl.ds(pl.multiple_of(start, LANES), LANES)
                return pltpu.roll(stage[number + i, :, span].astype(jnp.float32), roll, 1)

            @pl.when(send[begin + i] < ping_dev)
            def _():
                before = rolled(0)
                for b in range(blocks):
                    following = rolled(b + 1)
                    out[i, :, pl.ds(b * LANES, LANES)] = jnp.where(keep, before, following).astype(out.dtype)
                    before = following

            return 0

        lax.fori_loop(0, n, cut, 0)
        number += n


def turned(turn):
    g = turn - jnp.floor(turn + 0.5)
    u = g * g
    cosine = jnp.full_like(u, COS_TERMS[-1])
    for term in COS_TERMS[-2::-1]:
        cosine = cosine * u + term
    sine = jnp.full_like(u, SIN_TERMS[-1])
    for term in SIN_TERMS[-2::-1]:
        sine = sine * u + term
    return cosine, sine * g


def residue(number):
    modulus = jnp.float32(phase_modulus)
    return number - jnp.floor(number * jnp.float32(1.0 / phase_modulus) + 0.5) * modulus


def weights_kernel(spacing, pixels, table, where, cnt, me_ref, turn_ref, out, chirp):
    count = table.shape[0] // 3
    me = me_ref[0]
    step = pl.program_id(0)
    strip = 64
    strips = pixels // strip
    pairs = out.shape[1] // LANES
    inverse = jnp.float32(1.0 / phase_modulus)

    def rows_of(height):
        return lax.broadcasted_iota(jnp.int32, (height, LANES), 0).astype(jnp.float32)

    @pl.when(step == 0)
    def _():
        def one_strip(r, _):
            start = pl.multiple_of(r * strip, strip)
            x = residue(rows_of(strip) + start.astype(jnp.float32))
            cosine, sine = turned(residue(x * x) * inverse)
            chirp[0, pl.ds(start, strip), :] = cosine
            chirp[1, pl.ds(start, strip), :] = sine
            return 0

        lax.fori_loop(0, strips, one_strip, 0)

    lane = lax.broadcasted_iota(jnp.int32, (1, LANES), 1)
    second = lane >= 2 * C
    part = (lane // C) % 2
    channel = lane % C
    amount = jnp.full((1, LANES), cnt[me], jnp.int32).astype(jnp.float32)
    root = jnp.sqrt(jnp.float32(C) * amount)
    far = residue(rows_of(strips) * (2.0 * strip))
    for pair in range(pairs):
        bases, shifts, lives, backs = [], [], [], []
        for k in range(2):
            at = where[2 * (pairs * step + pair) + k]
            ping = table[at]
            bases.append(jnp.full((1, LANES), me * pixels - ping * spacing, jnp.int32))
            shifts.append(jnp.full((1, LANES), table[count + at], jnp.int32))
            lives.append(jnp.full((1, LANES), table[2 * count + at], jnp.int32))
            backs.append(jnp.full((1, LANES), turn_ref[ping], jnp.float32))
        pick = lambda both: jnp.where(second, both[1], both[0])
        base = residue(jnp.remainder(pick(bases) - 2 * channel, phase_modulus).astype(jnp.float32))
        turn = pick(shifts).astype(jnp.float32) * 0.125 + part.astype(jnp.float32) * 0.25
        scale = pick(lives).astype(jnp.float32) / root
        inner_real, inner_imag = turned(residue(2.0 * rows_of(strip) * base) * inverse)
        outer = residue(residue(far * base) + residue(base * base))
        outer_real, outer_imag = turned((outer * inverse + turn) - pick(backs))
        outer_real, outer_imag = outer_real * scale, outer_imag * scale
        column = pl.ds(pair * LANES, LANES)
        for s in range(strips):
            real, imag = outer_real[s : s + 1], outer_imag[s : s + 1]
            mid_real = inner_real * real - inner_imag * imag
            mid_imag = inner_real * imag + inner_imag * real
            here = pl.ds(s * strip, strip)
            chirp_real, chirp_imag = chirp[0, here, :], chirp[1, here, :]
            low = pl.ds(pixels + s * strip, strip)
            out[here, column] = (mid_real * chirp_real - mid_imag * chirp_imag).astype(out.dtype)
            out[low, column] = (mid_real * chirp_imag + mid_imag * chirp_real).astype(out.dtype)


def focus_kernel(sizes, weights, *refs):
    arrays = refs[: len(sizes)]
    total, out, window = refs[len(sizes) :]
    column = window.shape[1]
    here = pl.ds(pl.multiple_of(pl.program_id(0) * column, column), column)
    first = 0
    for array, size in zip(arrays, sizes):
        for i in range(size):
            window[pl.ds((first + i) * 2 * C, 2 * C), :] = array[i, :, here]
        first += size

    tall = weights.shape[0]
    piece = min(tall, PIECE)

    def one_piece(r, _):
        part = pl.ds(pl.multiple_of(r * piece, piece), piece)
        product = jnp.dot(weights[part, :], window[...], preferred_element_type=jnp.float32)
        out[part, :] = (total[part, :].astype(jnp.float32) + product).astype(out.dtype)
        return 0

    lax.fori_loop(0, tall // piece, one_piece, 0)


def params(mib):
    return pltpu.CompilerParams(vmem_limit_bytes=mib * MIB)


def swap(shard, by):
    return lax.ppermute(shard, "ping", [(i, i ^ by) for i in range(lax.axis_size("ping"))])


def after(value, *others):
    return lax.optimization_barrier((value, others))[0]


def exchanged(echoes, pairing, last_ping):
    owners, ranges = lax.axis_size("ping"), lax.axis_size("rng")
    channel_ids = jnp.arange(C, dtype=jnp.int32)
    front_pick = (pairing[:, 0, :, None] == channel_ids).astype(jnp.bfloat16)
    rear_pick = (pairing[:, 1, :, None] == channel_ids).astype(jnp.bfloat16)
    rear_rows = jnp.einsum("pkc,pzcr->pzkr", rear_pick, echoes, preferred_element_type=jnp.float32)
    inner_rows = jnp.einsum(
        "pkc,pzcr->pzkr", front_pick[1:], echoes[:-1], preferred_element_type=jnp.float32
    )
    lead_rows = jnp.einsum(
        "kc,zcr->zkr", front_pick[0], last_ping, preferred_element_type=jnp.float32
    )
    front_rows = jnp.concatenate([lead_rows[None], inner_rows], axis=0)
    cross_sum = jnp.sum(
        front_rows[:, 0] * rear_rows[:, 1] - front_rows[:, 1] * rear_rows[:, 0], axis=(1, 2)
    )
    front_energy = jnp.sum(front_rows * front_rows, axis=(1, 2, 3))
    rear_energy = jnp.sum(rear_rows * rear_rows, axis=(1, 2, 3))
    parts = jnp.stack([cross_sum, front_energy, rear_energy])
    if ranges & (ranges - 1):
        parts = lax.psum(parts, "rng")
    else:
        by = 1
        while by < ranges:
            parts = parts + lax.ppermute(parts, "rng", [(i, i ^ by) for i in range(ranges)])
            by *= 2
    mine = jnp.arange(owners, dtype=jnp.int32)[:, None] == lax.axis_index("ping")
    every = jnp.where(mine, parts[:, None, :], 0.0)
    return every + swap(every, 1)


def turns(every):
    every = every + (swap(every, 2) + (swap(every, 4) + swap(every, 6)))
    cross_sum, front_energy, rear_energy = every.reshape(3, -1)
    increment = cross_sum / (jnp.sqrt(front_energy * rear_energy) + small_value)
    order = jnp.arange(increment.shape[0], dtype=jnp.int32)
    track_turn = jnp.sum(jnp.where(order[None, :] <= order[:, None], increment[None, :], 0.0), axis=1)
    turn = track_turn * (1.0 / (2.0 * math.pi))
    return turn - jnp.floor(turn + 0.5)


def gather(send, flat, halo, spans, relayed=()):
    ping_dev, channels, width = flat.shape
    total = sum(n for _, n, _ in spans)
    return pl.pallas_call(
        functools.partial(gather_kernel, ping_dev, send.shape[0] // 2, spans),
        out_shape=[jax.ShapeDtypeStruct((n, channels, width), flat.dtype) for _, n, _ in spans],
        in_specs=[SMEM] + [ANY] * (2 + 2 * len(relayed)),
        out_specs=[VMEM] * len(spans),
        scratch_shapes=[
            pltpu.VMEM((total, channels, width + LANES), flat.dtype),
            pltpu.SemaphoreType.DMA((total, 2)),
        ],
        compiler_params=params(16),
        cost_estimate=SMALL,
        name="gather",
    )(send, flat, halo, *[a for pair in relayed for a in pair])


def chunked(chunks, counts, me, flat, halo, send, table, turn, moved, received, own, sibling, earlier):
    owners = lax.axis_size("ping")
    ping_dev, channels, width = flat.shape
    cap = -(-MOST // owners)
    room = 4 * cap
    pixels = earlier.shape[2]
    spacing = pixels * earlier.shape[0] // ping_dev

    def weights_of(places):
        slots = len(places)
        lanes = 2 * LANES if slots % 4 == 0 else LANES
        return pl.pallas_call(
            functools.partial(weights_kernel, spacing, pixels),
            grid=(slots * 2 * C // lanes,),
            in_specs=[SMEM] * 5,
            out_specs=pl.BlockSpec((2 * pixels, lanes), lambda i: (0, i)),
            out_shape=jax.ShapeDtypeStruct((2 * pixels, slots * 2 * C), jnp.bfloat16),
            scratch_shapes=[pltpu.VMEM((2, pixels, LANES), jnp.float32)],
            cost_estimate=SMALL,
            name="weights",
        )(table, np.asarray(places, np.int32), counts, me, turn)

    tile = pl.BlockSpec((2 * pixels, COLUMN), lambda i: (0, i))
    tiles = width // COLUMN
    inner = pl.BlockSpec((None, 2 * pixels, COLUMN), lambda i: (i, 0, 0))

    def focus(total, arrays, weight, final):
        sizes = [a.shape[0] for a in arrays]
        return pl.pallas_call(
            functools.partial(focus_kernel, sizes),
            grid=(tiles,),
            in_specs=[VMEM] * (1 + len(arrays)) + [tile if total.ndim == 2 else inner],
            out_specs=tile if final else inner,
            out_shape=jax.ShapeDtypeStruct((2 * pixels, width), earlier.dtype)
            if final
            else jax.ShapeDtypeStruct((tiles, 2 * pixels, COLUMN), jnp.float32),
            scratch_shapes=[pltpu.VMEM((sum(sizes) * 2 * C, COLUMN), jnp.bfloat16)],
            compiler_params=params(FOCUS_MIB),
            cost_estimate=SMALL,
            name="focus",
        )(weight, *arrays, total)

    starts = [sum(chunks[:c]) for c in range(len(chunks))]
    places = [[a * room + starts[c] + i for a in range(4) for i in range(n)] for c, n in enumerate(chunks)]
    places[0] = [4 * room + i for i in range(2 * cap)] + places[0]
    weights = [weights_of(p) for p in places]
    total = earlier.reshape(2 * pixels, width)
    history = [received]
    for c in range(len(chunks)):
        over_x, over_y = history[c]
        arrays = [over_x, over_y, swap(over_x, 1), swap(over_y, 1)]
        if c + 1 < len(chunks):
            coming = (swap(moved[0], 2), swap(moved[1], 4))
            if c + 2 < len(chunks):
                begin, n = starts[c + 2], chunks[c + 2]
                moved = gather(send, flat, halo, [(begin, n, 0), (room + begin, n, 1)], history[: min(c + 1, 2)])
        total = focus(total, ([own, sibling] if c == 0 else []) + arrays, weights[c], c == len(chunks) - 1)
        if c + 1 < len(chunks):
            coming, total, moved, send = lax.optimization_barrier((coming, total, moved, send))
            history.append(coming)
    return total.reshape(earlier.shape)


def paired_device(echoes, pairing, footprint, counts, offsets, earlier):
    owners, ranges = lax.axis_size("ping"), lax.axis_size("rng")
    tiles = footprint.shape[0]
    ping_dev, _, _, width = echoes.shape
    cap = -(-MOST // owners)
    room = 4 * cap
    base = owners * (owners // 2)
    flat = echoes.reshape(ping_dev, 2 * C, width)
    head = lax.slice_in_dim(flat, 0, LANES, axis=2)
    tail = lax.slice_in_dim(flat, width - LANES, width, axis=2)
    behind = lax.ppermute(head, "rng", [(i + 1, i) for i in range(ranges - 1)])
    ahead = lax.ppermute(tail, "rng", [(i, i + 1) for i in range(ranges - 1)])
    halo = jnp.where(jnp.arange(LANES) < BAND, behind, ahead)
    last_ping = passed_along(echoes[-1], "ping", 1)
    me = lax.axis_index("ping").astype(jnp.int32).reshape(1)
    whole = lambda *shape: jax.ShapeDtypeStruct(shape, jnp.int32)
    send, masks, shifts, chosen = pl.pallas_call(
        functools.partial(plan_kernel, owners, ping_dev, cap, tiles),
        out_shape=[
            whole(2 * (2 * room + 2 * cap)), whole(base + 2 * owners), whole(tiles * owners * ping_dev), whole(1)
        ],
        in_specs=[SMEM] * 4,
        out_specs=[SMEM] * 4,
        cost_estimate=SMALL,
        name="plan",
    )(footprint, counts, offsets, me)
    moved = gather(send, flat, halo, [(0, LEAD, 0), (room, LEAD, 1)])
    received = (swap(moved[0], 2), swap(moved[1], 4))
    turn = turns(exchanged(after(echoes, moved[0]), pairing, last_ping))
    later = after(send, moved[0])
    own, sibling = gather(later, flat, halo, [(2 * room, cap, None), (2 * room + cap, cap, None)])
    sibling = swap(sibling, 1)
    coming = gather(after(send, own), flat, halo, [(LEAD, LEAD, 0), (room + LEAD, LEAD, 1)])
    table = pl.pallas_call(
        functools.partial(places_kernel, owners, ping_dev, cap),
        out_shape=whole(3 * (4 * room + 2 * cap)),
        in_specs=[SMEM] * 6,
        out_specs=SMEM,
        cost_estimate=SMALL,
        name="places",
    )(footprint, counts, offsets, after(masks, own), shifts, me)
    return lax.switch(
        chosen[0],
        [functools.partial(chunked, v) for v in VARIANTS],
        counts, me, flat, halo, send, table, turn, coming, received, own, sibling, earlier,
    )


def per_device(echoes, pairing, footprint, counts, offsets, earlier):
    owners = lax.axis_size("ping")
    ping_dev = echoes.shape[0]
    paired = (
        owners == 8
        and footprint.shape[0] == owners
        and ping_dev <= 16
        and ping_dev & (ping_dev - 1) == 0
        and sum(VARIANTS[-1]) >= 4 * -(-MOST // owners)
    )
    device = paired_device if paired else general_device
    return device(echoes, pairing, footprint, counts, offsets, earlier)


def solution(mesh):
    return jax.shard_map(
        per_device,
        mesh=mesh,
        in_specs=(
            P("ping", None, None, "rng"),
            P("ping", None, None),
            P(),
            P(),
            P(),
            P("ping", None, None, "rng"),
        ),
        out_specs=P("ping", None, None, "rng"),
        check_vma=False,
    )
```

```python
import functools
import math

import jax
import jax.numpy as jnp
import numpy as np
from jax import lax
from jax.experimental import pallas as pl
from jax.experimental.pallas import tpu as pltpu
from jax.sharding import PartitionSpec as P

C = 32
X = 1024
BAND = 64
MOST = 48
TILE_DEV = 1
PING_DEV = 16


phase_modulus = 4099
small_value = 1e-06


def passed_along(shard, axis, by):
    length = lax.axis_size(axis)
    pairs = [(i, i + by) for i in range(length) if 0 <= i + by < length]
    return lax.ppermute(shard, axis, pairs)


def prefix(shard, axis, combine, identity):
    length, position = (lax.axis_size(axis), lax.axis_index(axis))
    everything = lax.all_gather(shard, axis)
    start = jnp.broadcast_to(jnp.asarray(identity, shard.dtype), shard.shape)

    def step(k, before):
        reached = k < position
        new = combine(before, everything[k])
        return jnp.where(reached, new, before)

    return lax.fori_loop(0, length, step, start)


def with_halo(cells, sides, width):
    for axis, dim in sides:
        count = lax.axis_size(axis)
        ends = count - 1
        head = lax.slice_in_dim(cells, 0, width, axis=dim)
        tail = lax.slice_in_dim(cells, cells.shape[dim] - width, cells.shape[dim], axis=dim)
        cells = jnp.concatenate(
            [
                lax.ppermute(tail, axis, [(i, (i + 1) % count) for i in range(ends)]),
                cells,
                lax.ppermute(head, axis, [((i + 1) % count, i) for i in range(ends)]),
            ],
            axis=dim,
        )
    return cells


def weight_matrix(tile_id, ping_ids, shift_ids, live_rows, tile_count):
    spacing = TILE_DEV * X // PING_DEV
    column = jnp.arange(ping_ids.shape[0] * 2 * C, dtype=jnp.int32)
    part_of = column // C % 2
    channel = column % C
    ping_cols = jnp.repeat(ping_ids, 2 * C)
    shift_cols = jnp.repeat(shift_ids, 2 * C)
    live_cols = jnp.repeat(live_rows, 2 * C)
    pixels = jnp.arange(X, dtype=jnp.int32)
    offset = tile_id * X - ping_cols * spacing - 2 * channel
    folded = jnp.remainder(pixels[:, None] + offset[None, :], phase_modulus)
    square = jnp.remainder(folded * folded, phase_modulus)
    phases = square.astype(jnp.float32) * (2.0 * math.pi / phase_modulus) + shift_cols.astype(
        jnp.float32
    )[None, :] * (math.pi / 4.0)
    scales = live_cols / jnp.sqrt(jnp.float32(C) * tile_count.astype(jnp.float32))
    cosine = jnp.cos(phases) * scales[None, :]
    sines = jnp.sin(phases) * scales[None, :]
    upper_rows = jnp.where(part_of[None, :] == 0, cosine, -sines)
    lower_rows = jnp.where(part_of[None, :] == 0, sines, cosine)
    return jnp.concatenate([upper_rows, lower_rows], axis=0).astype(jnp.bfloat16)


def focus_tile(received_data, received_labels):
    flat_rows = received_data.reshape((-1,) + received_data.shape[2:])
    flat_labels = received_labels.reshape(-1, 4)
    live_int = (flat_labels[:, 0] >= 0).astype(jnp.int32)
    ping_ids = flat_labels[:, 1]
    shift_ids = flat_labels[:, 2]
    tile_id = flat_labels[0, 3]
    tile_count = jnp.sum(live_int)
    block_len = flat_rows.shape[3]
    weights = weight_matrix(tile_id, ping_ids, shift_ids, live_int.astype(jnp.float32), tile_count)
    product = jnp.dot(weights, flat_rows.reshape(-1, block_len), preferred_element_type=jnp.float32)
    return product.reshape(2, X, block_len)


def focus(received):
    received_data, received_labels = received
    results = [focus_tile(received_data[:, 0], received_labels[:, 0])]
    return jnp.stack(results, axis=0)


def general_device(echoes, pairing, footprint, counts, offsets, earlier):
    ping_dev = echoes.shape[0]
    owners = lax.axis_size("ping")
    own_index = lax.axis_index("ping")
    channel_ids = jnp.arange(C, dtype=jnp.int32)
    front_pick = (pairing[:, 0, :, None] == channel_ids).astype(jnp.bfloat16)
    rear_pick = (pairing[:, 1, :, None] == channel_ids).astype(jnp.bfloat16)
    rear_rows = jnp.einsum("pkc,pzcr->pzkr", rear_pick, echoes, preferred_element_type=jnp.float32)
    inner_rows = jnp.einsum(
        "pkc,pzcr->pzkr", front_pick[1:], echoes[:-1], preferred_element_type=jnp.float32
    )
    last_ping = passed_along(echoes[-1], "ping", 1)
    lead_rows = jnp.einsum(
        "kc,zcr->zkr", front_pick[0], last_ping, preferred_element_type=jnp.float32
    )
    front_rows = jnp.concatenate([lead_rows[None], inner_rows], axis=0)
    cross_sum = jnp.sum(
        front_rows[:, 0] * rear_rows[:, 1] - front_rows[:, 1] * rear_rows[:, 0], axis=(1, 2)
    )
    front_energy = jnp.sum(front_rows * front_rows, axis=(1, 2, 3))
    rear_energy = jnp.sum(rear_rows * rear_rows, axis=(1, 2, 3))
    cross_sum, front_energy, rear_energy = lax.psum((cross_sum, front_energy, rear_energy), "rng")
    increment = cross_sum / (jnp.sqrt(front_energy * rear_energy) + small_value)
    running = jnp.cumsum(increment)
    before_turn = prefix(running[-1], "ping", jnp.add, jnp.float32(0.0))
    track_turn = before_turn + running
    cosine = jnp.cos(track_turn)[:, None, None]
    sines = jnp.sin(track_turn)[:, None, None]
    real_part = echoes[:, 0].astype(jnp.float32)
    imag_part = echoes[:, 1].astype(jnp.float32)
    corrected = jnp.stack(
        [real_part * cosine + imag_part * sines, imag_part * cosine - real_part * sines], axis=1
    ).astype(jnp.bfloat16)
    tile_total = footprint.shape[0]
    slot_cap = -(-MOST // owners)
    positions = jnp.arange(MOST, dtype=jnp.int32)
    in_list = positions[None, :] < counts[:, None]
    from_here = in_list & (footprint // ping_dev == own_index)
    order_here = jnp.cumsum(from_here.astype(jnp.int32), axis=1) - 1
    slot_ids = jnp.arange(slot_cap, dtype=jnp.int32)
    select = (from_here[:, None, :] & (order_here[:, None, :] == slot_ids[None, :, None])).astype(
        jnp.int32
    )
    place_ids = jnp.sum(select * (positions + 1)[None, None, :], axis=2) - 1
    local_ids = jnp.sum(select * (footprint % ping_dev)[:, None, :], axis=2)
    ping_ids = jnp.sum(select * footprint[:, None, :], axis=2)
    shift_ids = jnp.sum(select * offsets[:, None, :], axis=2)
    tile_ids = jnp.broadcast_to(jnp.arange(tile_total, dtype=jnp.int32)[:, None], place_ids.shape)
    labels = jnp.stack([place_ids, ping_ids, shift_ids, tile_ids], axis=2).reshape(
        owners, tile_total // owners, slot_cap, 4
    )
    block_len = corrected.shape[3]
    source = with_halo(corrected, (("rng", 3),), BAND)

    def cut_window(local_one, offset_one):
        return lax.dynamic_slice(
            source, (local_one, 0, 0, BAND + offset_one), (1, 2, C, block_len)
        )[0]

    outgoing = jax.vmap(cut_window)(local_ids.reshape(-1), shift_ids.reshape(-1))
    outgoing = outgoing.reshape((owners, tile_total // owners, slot_cap, 2, C, block_len))
    contribution = focus(
        (
            lax.all_to_all(outgoing, "ping", split_axis=0, concat_axis=0, tiled=True),
            lax.all_to_all(labels, "ping", split_axis=0, concat_axis=0, tiled=True),
        )
    )
    return (earlier.astype(jnp.float32) + contribution).astype(jnp.bfloat16)


LEAD = 4
CHUNKS = (4, 4, 4, 2)
EXTRA = ((2,), (4, 4))
UNIT = 8
STRIP = 64
STEP = 4
LANES = 128
SMALL = pl.CostEstimate(flops=1024, bytes_accessed=1024, transcendentals=0)
MIB = 1 << 20
COLUMN = 2048
PIECE = 512
TALL = 512
FOCUS_MIB = 56
SMEM = pl.BlockSpec(memory_space=pltpu.SMEM)
ANY = pl.BlockSpec(memory_space=pl.ANY)
VMEM = pl.BlockSpec(memory_space=pltpu.VMEM)
COS_TERMS = (
    1.0, -19.73920440673828, 64.93911743164062, -85.45014190673828, 60.16762924194336,
    -25.967599868774414, 6.528658390045166,
)
SIN_TERMS = (
    6.2831854820251465, -41.34170150756836, 81.60513305664062, -76.70301818847656, 42.02592849731445,
    -14.899847030639648, 3.2381374835968018,
)


def bit_count(mask):
    down = lax.shift_right_logical
    mask = mask - (down(mask, 1) & 0x55555555)
    mask = (mask & 0x33333333) + (down(mask, 2) & 0x33333333)
    mask = (mask + down(mask, 4)) & 0x0F0F0F0F
    mask = mask + down(mask, 8)
    return (mask + down(mask, 16)) & 0x3F


def each_bit(mask, place, visit):
    def body(_, carry):
        left, at = carry
        low = left & -left
        visit(at, bit_count(low - 1))
        return left ^ low, at + 1

    return lax.fori_loop(0, bit_count(mask), body, (mask, place))[1]


def link_list(masks, owners, s, axis, own, relay):
    chips = owners // 2
    near, other = (1, 4) if axis == 0 else (2, 2)
    base = owners * chips
    chip = s >> 1
    behind = s ^ other
    place = each_bit(masks[base + axis * owners + s], jnp.int32(0), lambda at, bit: own(at, chip ^ 3, bit))
    place = each_bit(masks[s * chips + (chip ^ near)], place, lambda at, bit: own(at, chip ^ near, bit))
    begin = jnp.maximum(place, 2 * LEAD)
    passed = masks[base + (1 - axis) * owners + behind]
    each_bit(passed, begin, lambda at, bit: relay(at, behind, chip ^ near, bit, at - begin))


def plan_kernel(owners, ping_dev, cap, tiles, fp, cnt, off, me_ref, _, send, masks, shifts, total, direct, over):
    chips = owners // 2
    bits = ping_dev.bit_length() - 1
    room = 4 * cap
    base = owners * chips
    pings = owners * ping_dev
    places = 2 * room + 2 * cap
    me = me_ref[0]

    def clear(i, _):
        masks[i] = 0
        return 0

    lax.fori_loop(0, base, clear, 0, unroll=8)

    def clear_send(i, _):
        send[i] = 0
        return 0

    lax.fori_loop(0, 2 * places, clear_send, 0, unroll=12)

    def one_tile(t, _):
        def entry(j, _):
            p = fp[t, j]
            at = (p >> bits) * chips + (t >> 1)
            masks[at] = masks[at] | lax.shift_left(jnp.int32(1), (p & (ping_dev - 1)) + (t & 1) * ping_dev)
            shifts[t * pings + p] = off[t, j]
            return 0

        return lax.fori_loop(0, cnt[t], entry, 0)

    lax.fori_loop(0, tiles, one_tile, 0)

    def far_of(s):
        return masks[s * chips + ((s >> 1) ^ 3)]

    def near_count(s, near):
        return bit_count(masks[s * chips + ((s >> 1) ^ near)])

    def begin(s, _):
        n = bit_count(far_of(s))
        direct[s] = near_count(s, 1)
        direct[owners + s] = near_count(s, 2)
        direct[2 * owners + s] = n
        over[s] = (n + 1) >> 1
        over[owners + s] = n - ((n + 1) >> 1)
        return 0

    lax.fori_loop(0, owners, begin, 0)

    def balance(k, _):
        s = k & (owners - 1)
        n = direct[2 * owners + s]
        by_x = jnp.maximum(direct[s] + over[owners + (s ^ 4)], direct[owners + (s ^ 2)] + over[owners + (s ^ 2)])
        by_y = jnp.maximum(direct[owners + s] + over[s ^ 2], direct[s ^ 4] + over[s ^ 4])
        want = (n + by_y - by_x + 1) >> 1
        want = jnp.minimum(jnp.maximum(want, jnp.maximum(n - cap, 0)), jnp.minimum(n, cap))
        over[s] = want
        over[owners + s] = n - want
        return 0

    lax.fori_loop(0, 3 * owners, balance, 0)

    def split(s, _):
        def take(_, carry):
            left, taken = carry
            low = left & -left
            return left ^ low, taken | low

        left, taken = lax.fori_loop(0, over[s], take, (far_of(s), jnp.int32(0)))
        masks[base + s] = taken
        masks[base + owners + s] = left
        return 0

    lax.fori_loop(0, owners, split, 0)

    def longest(s, most_yet):
        for axis, other in ((0, 4), (1, 2)):
            own = direct[axis * owners + s] + over[axis * owners + s]
            passed = over[(1 - axis) * owners + (s ^ other)]
            length = jnp.where(passed > 0, jnp.maximum(own, 2 * LEAD) + passed, own)
            most_yet = jnp.maximum(most_yet, length)
        return most_yet

    length = lax.fori_loop(0, owners, longest, jnp.int32(0))
    total[0] = length

    for axis in range(2):

        def own(at, chip, bit, axis=axis):
            ping = bit & (ping_dev - 1)
            tile = 2 * chip + (bit >> bits)
            send[axis * room + at] = ping
            send[places + axis * room + at] = shifts[tile * pings + me * ping_dev + ping]

        def relay(at, behind, chip, bit, i, axis=axis):
            send[axis * room + at] = ping_dev + i

        link_list(masks, owners, me, axis, own, relay)

    for k, tile in ((0, me), (1, me ^ 1)):

        def mine(j, at, k=k, tile=tile):
            p = fp[tile, j]
            here = (p >> bits) == me

            @pl.when(here)
            def _():
                send[2 * room + k * cap + at] = p & (ping_dev - 1)
                send[places + 2 * room + k * cap + at] = off[tile, j]

            return at + here.astype(jnp.int32)

        lax.fori_loop(0, cnt[tile], mine, jnp.int32(0))


def places_kernel(owners, ping_dev, cap, fp, cnt, masks, shifts, me_ref, _, table):
    bits = ping_dev.bit_length() - 1
    room = 4 * cap
    count = 4 * room + 2 * cap
    pings = owners * ping_dev
    me = me_ref[0]

    def clear(i, _):
        table[i] = 0
        return 0

    lax.fori_loop(0, 3 * count, clear, 0, unroll=12)

    def put(at, tile, ping):
        @pl.when(tile == me)
        def _():
            table[at] = ping
            table[count + at] = shifts[tile * pings + ping]
            table[2 * count + at] = 1

    for a, (axis, flip) in enumerate(((0, 2), (1, 4), (0, 3), (1, 5))):
        s = me ^ flip

        def own(at, chip, bit, a=a, s=s):
            put(a * room + at, 2 * chip + (bit >> bits), s * ping_dev + (bit & (ping_dev - 1)))

        def relay(at, behind, chip, bit, i, a=a):
            put(a * room + at, 2 * chip + (bit >> bits), behind * ping_dev + (bit & (ping_dev - 1)))

        link_list(masks, owners, s, axis, own, relay)

    for k, s in ((0, me), (1, me ^ 1)):

        def listed(j, at, k=k, s=s):
            p = fp[me, j]
            here = (p >> bits) == s

            @pl.when(here)
            def _():
                put(4 * room + k * cap + at, me, p)

            return at + here.astype(jnp.int32)

        lax.fori_loop(0, cnt[me], listed, jnp.int32(0))


def gather_kernel(ping_dev, places, spans, send, echoes, halo, _, *refs):
    outs, stage, sems = refs[-len(spans) - 2 : -2], refs[-2], refs[-1]
    sources = refs[: -len(spans) - 2]
    width = echoes.shape[2]
    blocks = width // LANES
    lane = lax.broadcasted_iota(jnp.int32, (2 * C, LANES), 1)
    jobs = [(begin + i, out, i, axis) for (begin, n, axis), out in zip(spans, outs) for i in range(n)]

    def copies(number):
        at, out, i, axis = jobs[number]
        index = send[at]
        here = jnp.minimum(index, ping_dev - 1)
        plain = [
            pltpu.make_async_copy(echoes.at[here], stage.at[number, :, pl.ds(0, width)], sems.at[number, 0]),
            pltpu.make_async_copy(halo.at[here], stage.at[number, :, pl.ds(width, LANES)], sems.at[number, 1]),
        ]
        if not sources:
            return [(None, plain)]
        groups = [(index < ping_dev, plain)]
        for k in range(len(sources) // 2):
            low = ping_dev + k * LEAD
            chosen = (index >= low) & (index < low + LEAD)
            source = sources[2 * k + 1 - axis].at[jnp.clip(index - low, 0, LEAD - 1)]
            groups.append((chosen, [pltpu.make_async_copy(source, out.at[i], sems.at[number, 0])]))
        return groups

    def act_on(number, act):
        for chosen, group in copies(number):
            if chosen is None:
                for copy in group:
                    act(copy)
            else:

                @pl.when(chosen)
                def _(group=group):
                    for copy in group:
                        act(copy)

    for number in range(len(jobs)):
        act_on(number, lambda copy: copy.start())
    for number in range(len(jobs)):
        act_on(number, lambda copy: copy.wait())

    number = 0
    for (begin, n, _), out in zip(spans, outs):

        def cut(i, _, begin=begin, out=out, number=number):
            offset = send[places + begin + i]
            within = offset & (LANES - 1)
            roll = (LANES - within) & (LANES - 1)
            keep = lane < LANES - within
            low = jnp.where(offset < 0, -LANES, 0)

            def rolled(b):
                start = low + b * LANES
                if b == 0:
                    start = jnp.where(start < 0, width, start)
                span = pl.ds(pl.multiple_of(start, LANES), LANES)
                return pltpu.roll(stage[number + i, :, span].astype(jnp.float32), roll, 1)

            @pl.when(send[begin + i] < ping_dev)
            def _():
                before = rolled(0)
                for b in range(blocks):
                    following = rolled(b + 1)
                    out[i, :, pl.ds(b * LANES, LANES)] = jnp.where(keep, before, following).astype(out.dtype)
                    before = following

            return 0

        lax.fori_loop(0, n, cut, 0)
        number += n


def turned(turn):
    g = turn - jnp.floor(turn + 0.5)
    u = g * g
    cosine = jnp.full_like(u, COS_TERMS[-1])
    for term in COS_TERMS[-2::-1]:
        cosine = cosine * u + term
    sine = jnp.full_like(u, SIN_TERMS[-1])
    for term in SIN_TERMS[-2::-1]:
        sine = sine * u + term
    return cosine, sine * g


def residue(number):
    modulus = jnp.float32(phase_modulus)
    return number - jnp.floor(number * jnp.float32(1.0 / phase_modulus) + 0.5) * modulus


def live_units(count):
    return jnp.maximum((count + UNIT - 1) // UNIT, 1)


def weights_kernel(spacing, pixels, slots, table, where, cnt, me_ref, turn_ref, _, out, mark, chirp, inner, outer, columns, known):
    count = table.shape[0] // 3
    me = me_ref[0]
    step = pl.program_id(0)
    strip = inner.shape[1]
    strips = pixels // strip
    width = out.shape[1]
    inverse = jnp.float32(1.0 / phase_modulus)
    wide = 4 * LANES

    def rows_of(height, across):
        return lax.broadcasted_iota(jnp.int32, (height, across), 0).astype(jnp.float32)

    @pl.when(step == 0)
    def _():
        mark[...] = jnp.zeros_like(mark)
        tall = min(pixels, 256)

        def one_part(r, _):
            start = pl.multiple_of(r * tall, tall)
            x = residue(rows_of(tall, LANES) + start.astype(jnp.float32))
            cosine, sine = turned(residue(x * x) * inverse)
            chirp[0, pl.ds(start, tall), :] = cosine
            chirp[1, pl.ds(start, tall), :] = sine
            return 0

        lax.fori_loop(0, pixels // tall, one_part, 0)
        columns[...] = jnp.zeros_like(columns)
        lane = lax.broadcasted_iota(jnp.int32, (1, LANES), 1)

        def note(i, at):
            live = table[2 * count + where[i]]

            @pl.when(live > 0)
            def _():
                ping = table[where[i]]
                half = (lane >= 2 * C) == ((at & 1) == 1)
                span = pl.ds(pl.multiple_of((at >> 1) * LANES, LANES), LANES)
                distance = (me * pixels - ping * spacing).astype(jnp.float32)
                turn = table[count + where[i]].astype(jnp.float32) * 0.125 - turn_ref[ping]
                for row, value in ((0, distance), (1, turn), (2, jnp.float32(1.0))):
                    columns[row : row + 1, span] = jnp.where(half, value, columns[row : row + 1, span])

            return at + live

        known[0] = lax.fori_loop(0, slots, note, jnp.int32(0))
        amount = jnp.full((1, wide), cnt[me], jnp.int32).astype(jnp.float32)
        root = jnp.sqrt(jnp.float32(C) * amount)
        lane = lax.broadcasted_iota(jnp.int32, (1, wide), 1)
        channel = (lane % C).astype(jnp.float32)
        part = ((lane // C) % 2).astype(jnp.float32)

        def angles(i, _):
            span = pl.ds(pl.multiple_of(i * wide, wide), wide)
            base = residue(columns[0:1, span] - 2.0 * channel)
            cosine, sine = turned(residue(2.0 * rows_of(strip, wide) * base) * inverse)
            inner[0, :, span] = cosine
            inner[1, :, span] = sine
            far = residue(rows_of(strips, wide) * (2.0 * strip))
            angle = residue(residue(far * base) + residue(base * base)) * inverse
            cosine, sine = turned(angle + (columns[1:2, span] + 0.25 * part))
            scale = columns[2:3, span] / root
            outer[0, :, span] = cosine * scale
            outer[1, :, span] = sine * scale
            return 0

        lax.fori_loop(0, (UNIT * live_units(known[0]) * 2 * C) // wide, angles, 0)

    @pl.when(STEP * step < UNIT * live_units(known[0]))
    def _():
        for pair in range(width // LANES):
            span = pl.ds(pl.multiple_of(step * width + pair * LANES, LANES), LANES)
            column = pl.ds(pair * LANES, LANES)
            inner_real, inner_imag = inner[0, :, span], inner[1, :, span]
            outer_real, outer_imag = outer[0, :, span], outer[1, :, span]
            for s in range(strips):
                real, imag = outer_real[s : s + 1], outer_imag[s : s + 1]
                mid_real = inner_real * real - inner_imag * imag
                mid_imag = inner_real * imag + inner_imag * real
                here = pl.ds(s * strip, strip)
                chirp_real, chirp_imag = chirp[0, here, :], chirp[1, here, :]
                low = pl.ds(pixels + s * strip, strip)
                out[here, column] = (mid_real * chirp_real - mid_imag * chirp_imag).astype(out.dtype)
                out[low, column] = (mid_real * chirp_imag + mid_imag * chirp_real).astype(out.dtype)


def focus_kernel(sizes, table, where, _, weights, *refs):
    arrays = refs[: len(sizes)]
    total, out, mark, window, sems, known = refs[len(sizes) :]
    count = table.shape[0] // 3
    rows = 2 * C
    column = out.shape[1]
    here = pl.ds(pl.multiple_of(pl.program_id(1) * column, column), column)

    def window_copy(array, i, at):
        place = pl.ds(pl.multiple_of(at * rows, rows), rows)
        return pltpu.make_async_copy(array.at[i], window.at[place, :], sems.at[at])

    @pl.when((pl.program_id(0) == 0) & (pl.program_id(1) == 0))
    def _():
        mark[...] = jnp.zeros_like(mark)
        at, slot = jnp.int32(0), 0
        for array, size in zip(arrays, sizes):
            for i in range(size):
                live = table[2 * count + where[slot]]

                @pl.when(live > 0)
                def _(array=array, i=i, at=at):
                    window_copy(array, i, at).start()

                at, slot = at + live, slot + 1
        known[0] = at

        def blank(i, _):
            window[pl.ds(pl.multiple_of(i * rows, rows), rows), :] = jnp.zeros((rows, window.shape[1]), window.dtype)
            return 0

        lax.fori_loop(at, UNIT * live_units(at), blank, 0)

        def ready(i, _):
            window_copy(arrays[0], 0, i).wait()
            return 0

        lax.fori_loop(0, at, ready, 0)

    tall = weights.shape[0]
    piece = min(tall, PIECE)
    for units in range(1, weights.shape[1] // (UNIT * rows) + 1):

        @pl.when(live_units(known[0]) == units)
        def _(units=units):
            deep = pl.ds(0, units * UNIT * rows)

            def one_piece(r, _):
                part = pl.ds(pl.multiple_of(r * piece, piece), piece)
                product = jnp.dot(weights[part, deep], window[deep, here], preferred_element_type=jnp.float32)
                out[part, :] = (total[part, :].astype(jnp.float32) + product).astype(out.dtype)
                return 0

            lax.fori_loop(0, tall // piece, one_piece, 0)


def params(mib):
    return pltpu.CompilerParams(vmem_limit_bytes=mib * MIB)


def swap(shard, by):
    return lax.ppermute(shard, "ping", [(i, i ^ by) for i in range(lax.axis_size("ping"))])


def correlated(echoes, pairing, last_ping):
    channel_ids = jnp.arange(C, dtype=jnp.int32)
    front_pick = (pairing[:, 0, :, None] == channel_ids).astype(jnp.bfloat16)
    rear_pick = (pairing[:, 1, :, None] == channel_ids).astype(jnp.bfloat16)
    rear_rows = jnp.einsum("pkc,pzcr->pzkr", rear_pick, echoes, preferred_element_type=jnp.float32)
    inner_rows = jnp.einsum(
        "pkc,pzcr->pzkr", front_pick[1:], echoes[:-1], preferred_element_type=jnp.float32
    )
    lead_rows = jnp.einsum(
        "kc,zcr->zkr", front_pick[0], last_ping, preferred_element_type=jnp.float32
    )
    front_rows = jnp.concatenate([lead_rows[None], inner_rows], axis=0)
    cross_sum = jnp.sum(
        front_rows[:, 0] * rear_rows[:, 1] - front_rows[:, 1] * rear_rows[:, 0], axis=(1, 2)
    )
    front_energy = jnp.sum(front_rows * front_rows, axis=(1, 2, 3))
    rear_energy = jnp.sum(rear_rows * rear_rows, axis=(1, 2, 3))
    return jnp.stack([cross_sum, front_energy, rear_energy])


def over_ranges(parts):
    ranges = lax.axis_size("rng")
    if ranges & (ranges - 1):
        return lax.psum(parts, "rng")
    others = [lax.ppermute(parts, "rng", [(i, i ^ by) for i in range(ranges)]) for by in range(1, ranges)]
    return functools.reduce(jnp.add, others, parts)


def over_chip(parts):
    owners = lax.axis_size("ping")
    mine = jnp.arange(owners, dtype=jnp.int32)[:, None] == lax.axis_index("ping")
    every = jnp.where(mine, parts[:, None, :], 0.0)
    return every + swap(every, 1)


def turns(every):
    every = every + (swap(every, 2) + (swap(every, 4) + swap(every, 6)))
    cross_sum, front_energy, rear_energy = every.reshape(3, -1)
    increment = cross_sum / (jnp.sqrt(front_energy * rear_energy) + small_value)
    order = jnp.arange(increment.shape[0], dtype=jnp.int32)
    track_turn = jnp.sum(jnp.where(order[None, :] <= order[:, None], increment[None, :], 0.0), axis=1)
    turn = track_turn * (1.0 / (2.0 * math.pi))
    return turn - jnp.floor(turn + 0.5)


def gather(send, flat, halo, spans, relayed=(), tie=None):
    ping_dev, channels, width = flat.shape
    total = sum(n for _, n, _ in spans)
    return pl.pallas_call(
        functools.partial(gather_kernel, ping_dev, send.shape[0] // 2, spans),
        out_shape=[jax.ShapeDtypeStruct((n, channels, width), flat.dtype) for _, n, _ in spans],
        in_specs=[SMEM] + [ANY] * (3 + 2 * len(relayed)),
        out_specs=[VMEM] * len(spans),
        scratch_shapes=[
            pltpu.VMEM((total, channels, width + LANES), flat.dtype),
            pltpu.SemaphoreType.DMA((total, 2)),
        ],
        compiler_params=params(16),
        cost_estimate=SMALL,
        name="gather",
    )(send, flat, halo, send if tie is None else tie, *[a for pair in relayed for a in pair])


def whole_units(slots):
    return -(-slots // UNIT) * UNIT


def weights_of(places, table, counts, me, turn, pixels, spacing, tie):
    slots = whole_units(len(places))
    lanes = STEP * 2 * C
    return pl.pallas_call(
        functools.partial(weights_kernel, spacing, pixels, len(places)),
        grid=(slots // STEP,),
        in_specs=[SMEM] * 5 + [ANY],
        out_specs=[pl.BlockSpec((2 * pixels, lanes), lambda i: (0, i)), pl.BlockSpec((8, LANES), lambda i: (0, 0))],
        out_shape=[
            jax.ShapeDtypeStruct((2 * pixels, slots * 2 * C), jnp.bfloat16),
            jax.ShapeDtypeStruct((8, LANES), jnp.float32),
        ],
        scratch_shapes=[
            pltpu.VMEM((2, pixels, LANES), jnp.float32),
            pltpu.VMEM((2, STRIP, slots * 2 * C), jnp.float32),
            pltpu.VMEM((2, pixels // STRIP, slots * 2 * C), jnp.float32),
            pltpu.VMEM((8, slots * 2 * C), jnp.float32),
            pltpu.SMEM((1,), jnp.int32),
        ],
        cost_estimate=SMALL,
        name="weights",
    )(table, np.asarray(places, np.int32), counts, me, turn, tie)


def add_windows(total, arrays, places, weight, table, tie, kind=None):
    height, deep = weight.shape
    width = arrays[0].shape[2]
    flat = pl.BlockSpec((TALL, COLUMN), lambda r, i: (r, i))
    inner = pl.BlockSpec((None, TALL, COLUMN), lambda r, i: (i, r, 0))
    return pl.pallas_call(
        functools.partial(focus_kernel, [a.shape[0] for a in arrays]),
        grid=(height // TALL, width // COLUMN),
        in_specs=[SMEM] * 2
        + [ANY, pl.BlockSpec((TALL, deep), lambda r, i: (r, 0))]
        + [ANY] * len(arrays)
        + [flat if total.ndim == 2 else inner],
        out_specs=[inner if kind is None else flat, pl.BlockSpec((8, LANES), lambda r, i: (0, 0))],
        out_shape=[
            jax.ShapeDtypeStruct((width // COLUMN, height, COLUMN), jnp.float32)
            if kind is None
            else jax.ShapeDtypeStruct((height, width), kind),
            jax.ShapeDtypeStruct((8, LANES), jnp.float32),
        ],
        scratch_shapes=[
            pltpu.VMEM((deep, width), jnp.bfloat16),
            pltpu.SemaphoreType.DMA((deep // (2 * C),)),
            pltpu.SMEM((1,), jnp.int32),
        ],
        compiler_params=params(FOCUS_MIB),
        cost_estimate=SMALL,
        name="focus",
    )(table, np.asarray(places, np.int32), tie, weight, *arrays, total)


def places_of(begin, n, room):
    return [a * room + begin + i for a in range(4) for i in range(n)]


def with_sibling(pair):
    return [pair[0], pair[1], swap(pair[0], 1), swap(pair[1], 1)]


def added_more(stage, begin, total, length, flat, halo, send, table, turn, counts, me, over, pixels, spacing):
    if stage == len(EXTRA):
        return total
    room = 4 * -(-MOST // lax.axis_size("ping"))

    def more(total):
        at = begin
        for n in EXTRA[stage]:
            cut = gather(send, flat, halo, [(at, n, 0), (room + at, n, 1)], over[:2], table)
            places = places_of(at, n, room)
            weight, _ = weights_of(places, table, counts, me, turn, pixels, spacing, cut[0])
            pair = (swap(cut[0], 2), swap(cut[1], 4))
            total, _ = add_windows(total, with_sibling(pair), places, weight, table, cut[0])
            at += n
        return added_more(stage + 1, at, total, length, flat, halo, send, table, turn, counts, me, over, pixels, spacing)

    return lax.cond(length > begin, more, lambda total: total, total)


def paired_device(echoes, pairing, footprint, counts, offsets, earlier):
    owners, ranges = lax.axis_size("ping"), lax.axis_size("rng")
    tiles = footprint.shape[0]
    ping_dev, _, _, width = echoes.shape
    cap = -(-MOST // owners)
    room = 4 * cap
    base = owners * (owners // 2)
    last_ping = passed_along(echoes[-1], "ping", 1)
    flat = echoes.reshape(ping_dev, 2 * C, width)
    head = lax.slice_in_dim(flat, 0, LANES, axis=2)
    tail = lax.slice_in_dim(flat, width - LANES, width, axis=2)
    behind = lax.ppermute(head, "rng", [(i + 1, i) for i in range(ranges - 1)])
    ahead = lax.ppermute(tail, "rng", [(i, i + 1) for i in range(ranges - 1)])
    halo = jnp.where(jnp.arange(LANES) < BAND, behind, ahead)
    parts = correlated(echoes, pairing, last_ping)
    me = lax.axis_index("ping").astype(jnp.int32).reshape(1)
    whole = lambda *shape: jax.ShapeDtypeStruct(shape, jnp.int32)
    send, masks, shifts, length = pl.pallas_call(
        functools.partial(plan_kernel, owners, ping_dev, cap, tiles),
        out_shape=[
            whole(2 * (2 * room + 2 * cap)), whole(base + 2 * owners), whole(tiles * owners * ping_dev), whole(1)
        ],
        in_specs=[SMEM] * 4 + [ANY],
        out_specs=[SMEM] * 4,
        scratch_shapes=[pltpu.SMEM((3 * owners,), jnp.int32), pltpu.SMEM((2 * owners,), jnp.int32)],
        cost_estimate=SMALL,
        name="plan",
    )(footprint, counts, offsets, me, parts)
    summed = over_ranges(parts)

    def spans_of(c):
        begin = sum(CHUNKS[:c])
        return [(begin, CHUNKS[c], 0), (room + begin, CHUNKS[c], 1)]

    turn = turns(over_chip(summed))
    moved = gather(send, flat, halo, spans_of(0), (), turn)
    over = [(swap(moved[0], 2), swap(moved[1], 4))]
    own, sibling = gather(send, flat, halo, [(2 * room, cap, None), (2 * room + cap, cap, None)], (), moved[0])
    table = pl.pallas_call(
        functools.partial(places_kernel, owners, ping_dev, cap),
        out_shape=whole(3 * (4 * room + 2 * cap)),
        in_specs=[SMEM] * 5 + [ANY],
        out_specs=SMEM,
        cost_estimate=SMALL,
        name="places",
    )(footprint, counts, masks, shifts, me, own)
    moved = gather(send, flat, halo, spans_of(1), (), table)
    over.append((swap(moved[0], 2), swap(moved[1], 4)))
    pixels = earlier.shape[2]
    spacing = pixels * earlier.shape[0] // ping_dev
    places = [places_of(sum(CHUNKS[:c]), n, room) for c, n in enumerate(CHUNKS)]
    early = [4 * room + i for i in range(2 * cap)] + places[0] + places[1]
    late = places[2] + places[3]
    early_weights, mark = weights_of(early, table, counts, me, turn, pixels, spacing, moved[0])
    over[0], mark = lax.optimization_barrier((over[0], mark))
    arrays = [own, swap(sibling, 1)] + with_sibling(over[0])
    moved = gather(send, flat, halo, spans_of(2), over[:1], mark)
    over.append((swap(moved[0], 2), swap(moved[1], 4)))
    late_weights, mark = weights_of(late, table, counts, me, turn, pixels, spacing, moved[0])
    over[1], mark = lax.optimization_barrier((over[1], mark))
    arrays = arrays + with_sibling(over[1])
    moved = gather(send, flat, halo, spans_of(3), over[:2], mark)
    over.append((swap(moved[0], 2), swap(moved[1], 4)))
    total, mark = add_windows(earlier.reshape(2 * pixels, width), arrays, early, early_weights, table, moved[0])
    total = added_more(
        0, sum(CHUNKS), total, length[0], flat, halo, send, table, turn, counts, me, over[:2], pixels, spacing
    )
    over[2], over[3], mark = lax.optimization_barrier((over[2], over[3], mark))
    arrays = with_sibling(over[2]) + with_sibling(over[3])
    total, _ = add_windows(total, arrays, late, late_weights, table, mark, earlier.dtype)
    return total.reshape(earlier.shape)


def per_device(echoes, pairing, footprint, counts, offsets, earlier):
    owners = lax.axis_size("ping")
    ping_dev = echoes.shape[0]
    paired = (
        owners == 8
        and footprint.shape[0] == owners
        and ping_dev <= 16
        and ping_dev & (ping_dev - 1) == 0
        and sum(CHUNKS) + sum(map(sum, EXTRA)) >= 4 * -(-MOST // owners)
    )
    device = paired_device if paired else general_device
    return device(echoes, pairing, footprint, counts, offsets, earlier)


def solution(mesh):
    return jax.shard_map(
        per_device,
        mesh=mesh,
        in_specs=(
            P("ping", None, None, "rng"),
            P("ping", None, None),
            P(),
            P(),
            P(),
            P("ping", None, None, "rng"),
        ),
        out_specs=P("ping", None, None, "rng"),
        check_vma=False,
    )
```

```python
import functools
import math

import jax
import jax.numpy as jnp
import numpy as np
from jax import lax
from jax.experimental import pallas as pl
from jax.experimental.pallas import tpu as pltpu
from jax.sharding import PartitionSpec as P

C = 32
X = 1024
BAND = 64
MOST = 48
TILE_DEV = 1
PING_DEV = 16


phase_modulus = 4099
small_value = 1e-06


def passed_along(shard, axis, by):
    length = lax.axis_size(axis)
    pairs = [(i, i + by) for i in range(length) if 0 <= i + by < length]
    return lax.ppermute(shard, axis, pairs)


def prefix(shard, axis, combine, identity):
    length, position = (lax.axis_size(axis), lax.axis_index(axis))
    everything = lax.all_gather(shard, axis)
    start = jnp.broadcast_to(jnp.asarray(identity, shard.dtype), shard.shape)

    def step(k, before):
        reached = k < position
        new = combine(before, everything[k])
        return jnp.where(reached, new, before)

    return lax.fori_loop(0, length, step, start)


def with_halo(cells, sides, width):
    for axis, dim in sides:
        count = lax.axis_size(axis)
        ends = count - 1
        head = lax.slice_in_dim(cells, 0, width, axis=dim)
        tail = lax.slice_in_dim(cells, cells.shape[dim] - width, cells.shape[dim], axis=dim)
        cells = jnp.concatenate(
            [
                lax.ppermute(tail, axis, [(i, (i + 1) % count) for i in range(ends)]),
                cells,
                lax.ppermute(head, axis, [((i + 1) % count, i) for i in range(ends)]),
            ],
            axis=dim,
        )
    return cells


def weight_matrix(tile_id, ping_ids, shift_ids, live_rows, tile_count):
    spacing = TILE_DEV * X // PING_DEV
    column = jnp.arange(ping_ids.shape[0] * 2 * C, dtype=jnp.int32)
    part_of = column // C % 2
    channel = column % C
    ping_cols = jnp.repeat(ping_ids, 2 * C)
    shift_cols = jnp.repeat(shift_ids, 2 * C)
    live_cols = jnp.repeat(live_rows, 2 * C)
    pixels = jnp.arange(X, dtype=jnp.int32)
    offset = tile_id * X - ping_cols * spacing - 2 * channel
    folded = jnp.remainder(pixels[:, None] + offset[None, :], phase_modulus)
    square = jnp.remainder(folded * folded, phase_modulus)
    phases = square.astype(jnp.float32) * (2.0 * math.pi / phase_modulus) + shift_cols.astype(
        jnp.float32
    )[None, :] * (math.pi / 4.0)
    scales = live_cols / jnp.sqrt(jnp.float32(C) * tile_count.astype(jnp.float32))
    cosine = jnp.cos(phases) * scales[None, :]
    sines = jnp.sin(phases) * scales[None, :]
    upper_rows = jnp.where(part_of[None, :] == 0, cosine, -sines)
    lower_rows = jnp.where(part_of[None, :] == 0, sines, cosine)
    return jnp.concatenate([upper_rows, lower_rows], axis=0).astype(jnp.bfloat16)


def focus_tile(received_data, received_labels):
    flat_rows = received_data.reshape((-1,) + received_data.shape[2:])
    flat_labels = received_labels.reshape(-1, 4)
    live_int = (flat_labels[:, 0] >= 0).astype(jnp.int32)
    ping_ids = flat_labels[:, 1]
    shift_ids = flat_labels[:, 2]
    tile_id = flat_labels[0, 3]
    tile_count = jnp.sum(live_int)
    block_len = flat_rows.shape[3]
    weights = weight_matrix(tile_id, ping_ids, shift_ids, live_int.astype(jnp.float32), tile_count)
    product = jnp.dot(weights, flat_rows.reshape(-1, block_len), preferred_element_type=jnp.float32)
    return product.reshape(2, X, block_len)


def focus(received):
    received_data, received_labels = received
    results = [focus_tile(received_data[:, 0], received_labels[:, 0])]
    return jnp.stack(results, axis=0)


def general_device(echoes, pairing, footprint, counts, offsets, earlier):
    ping_dev = echoes.shape[0]
    owners = lax.axis_size("ping")
    own_index = lax.axis_index("ping")
    channel_ids = jnp.arange(C, dtype=jnp.int32)
    front_pick = (pairing[:, 0, :, None] == channel_ids).astype(jnp.bfloat16)
    rear_pick = (pairing[:, 1, :, None] == channel_ids).astype(jnp.bfloat16)
    rear_rows = jnp.einsum("pkc,pzcr->pzkr", rear_pick, echoes, preferred_element_type=jnp.float32)
    inner_rows = jnp.einsum(
        "pkc,pzcr->pzkr", front_pick[1:], echoes[:-1], preferred_element_type=jnp.float32
    )
    last_ping = passed_along(echoes[-1], "ping", 1)
    lead_rows = jnp.einsum(
        "kc,zcr->zkr", front_pick[0], last_ping, preferred_element_type=jnp.float32
    )
    front_rows = jnp.concatenate([lead_rows[None], inner_rows], axis=0)
    cross_sum = jnp.sum(
        front_rows[:, 0] * rear_rows[:, 1] - front_rows[:, 1] * rear_rows[:, 0], axis=(1, 2)
    )
    front_energy = jnp.sum(front_rows * front_rows, axis=(1, 2, 3))
    rear_energy = jnp.sum(rear_rows * rear_rows, axis=(1, 2, 3))
    cross_sum, front_energy, rear_energy = lax.psum((cross_sum, front_energy, rear_energy), "rng")
    increment = cross_sum / (jnp.sqrt(front_energy * rear_energy) + small_value)
    running = jnp.cumsum(increment)
    before_turn = prefix(running[-1], "ping", jnp.add, jnp.float32(0.0))
    track_turn = before_turn + running
    cosine = jnp.cos(track_turn)[:, None, None]
    sines = jnp.sin(track_turn)[:, None, None]
    real_part = echoes[:, 0].astype(jnp.float32)
    imag_part = echoes[:, 1].astype(jnp.float32)
    corrected = jnp.stack(
        [real_part * cosine + imag_part * sines, imag_part * cosine - real_part * sines], axis=1
    ).astype(jnp.bfloat16)
    tile_total = footprint.shape[0]
    slot_cap = -(-MOST // owners)
    positions = jnp.arange(MOST, dtype=jnp.int32)
    in_list = positions[None, :] < counts[:, None]
    from_here = in_list & (footprint // ping_dev == own_index)
    order_here = jnp.cumsum(from_here.astype(jnp.int32), axis=1) - 1
    slot_ids = jnp.arange(slot_cap, dtype=jnp.int32)
    select = (from_here[:, None, :] & (order_here[:, None, :] == slot_ids[None, :, None])).astype(
        jnp.int32
    )
    place_ids = jnp.sum(select * (positions + 1)[None, None, :], axis=2) - 1
    local_ids = jnp.sum(select * (footprint % ping_dev)[:, None, :], axis=2)
    ping_ids = jnp.sum(select * footprint[:, None, :], axis=2)
    shift_ids = jnp.sum(select * offsets[:, None, :], axis=2)
    tile_ids = jnp.broadcast_to(jnp.arange(tile_total, dtype=jnp.int32)[:, None], place_ids.shape)
    labels = jnp.stack([place_ids, ping_ids, shift_ids, tile_ids], axis=2).reshape(
        owners, tile_total // owners, slot_cap, 4
    )
    block_len = corrected.shape[3]
    source = with_halo(corrected, (("rng", 3),), BAND)

    def cut_window(local_one, offset_one):
        return lax.dynamic_slice(
            source, (local_one, 0, 0, BAND + offset_one), (1, 2, C, block_len)
        )[0]

    outgoing = jax.vmap(cut_window)(local_ids.reshape(-1), shift_ids.reshape(-1))
    outgoing = outgoing.reshape((owners, tile_total // owners, slot_cap, 2, C, block_len))
    contribution = focus(
        (
            lax.all_to_all(outgoing, "ping", split_axis=0, concat_axis=0, tiled=True),
            lax.all_to_all(labels, "ping", split_axis=0, concat_axis=0, tiled=True),
        )
    )
    return (earlier.astype(jnp.float32) + contribution).astype(jnp.bfloat16)


LEAD = 4
CHUNKS = (4, 4, 4, 2)
EXTRA = ((2,), (4, 4))
UNIT = 4
STRIP = 64
STEP = UNIT
LANES = 128
SMALL = pl.CostEstimate(flops=1024, bytes_accessed=1024, transcendentals=0)
MIB = 1 << 20
COLUMN = 2048
PIECE = 512
TALL = 512
FOCUS_MIB = 56
SMEM = pl.BlockSpec(memory_space=pltpu.SMEM)
ANY = pl.BlockSpec(memory_space=pl.ANY)
VMEM = pl.BlockSpec(memory_space=pltpu.VMEM)
COS_TERMS = (
    1.0, -19.73920440673828, 64.93911743164062, -85.45014190673828, 60.16762924194336,
    -25.967599868774414, 6.528658390045166,
)
SIN_TERMS = (
    6.2831854820251465, -41.34170150756836, 81.60513305664062, -76.70301818847656, 42.02592849731445,
    -14.899847030639648, 3.2381374835968018,
)


def bit_count(mask):
    down = lax.shift_right_logical
    mask = mask - (down(mask, 1) & 0x55555555)
    mask = (mask & 0x33333333) + (down(mask, 2) & 0x33333333)
    mask = (mask + down(mask, 4)) & 0x0F0F0F0F
    mask = mask + down(mask, 8)
    return (mask + down(mask, 16)) & 0x3F


def each_bit(mask, place, visit):
    def body(_, carry):
        left, at = carry
        low = left & -left
        visit(at, bit_count(low - 1))
        return left ^ low, at + 1

    return lax.fori_loop(0, bit_count(mask), body, (mask, place))[1]


def link_list(masks, owners, s, axis, own, relay):
    chips = owners // 2
    near, other = (1, 4) if axis == 0 else (2, 2)
    base = owners * chips
    chip = s >> 1
    behind = s ^ other
    place = each_bit(masks[base + axis * owners + s], jnp.int32(0), lambda at, bit: own(at, chip ^ 3, bit))
    place = each_bit(masks[s * chips + (chip ^ near)], place, lambda at, bit: own(at, chip ^ near, bit))
    begin = jnp.maximum(place, 2 * LEAD)
    passed = masks[base + (1 - axis) * owners + behind]
    each_bit(passed, begin, lambda at, bit: relay(at, behind, chip ^ near, bit, at - begin))


def plan_kernel(owners, ping_dev, cap, tiles, fp, cnt, off, me_ref, send, masks, shifts, total, direct, over):
    chips = owners // 2
    bits = ping_dev.bit_length() - 1
    room = 4 * cap
    base = owners * chips
    pings = owners * ping_dev
    places = 2 * room + 2 * cap
    me = me_ref[0]

    def clear(i, _):
        masks[i] = 0
        return 0

    lax.fori_loop(0, base, clear, 0, unroll=8)

    def clear_send(i, _):
        send[i] = 0
        return 0

    lax.fori_loop(0, 2 * places, clear_send, 0, unroll=12)

    def one_tile(t, _):
        def entry(j, _):
            p = fp[t, j]
            at = (p >> bits) * chips + (t >> 1)
            masks[at] = masks[at] | lax.shift_left(jnp.int32(1), (p & (ping_dev - 1)) + (t & 1) * ping_dev)
            shifts[t * pings + p] = off[t, j]
            return 0

        return lax.fori_loop(0, cnt[t], entry, 0)

    lax.fori_loop(0, tiles, one_tile, 0)

    def far_of(s):
        return masks[s * chips + ((s >> 1) ^ 3)]

    def near_count(s, near):
        return bit_count(masks[s * chips + ((s >> 1) ^ near)])

    def begin(s, _):
        n = bit_count(far_of(s))
        direct[s] = near_count(s, 1)
        direct[owners + s] = near_count(s, 2)
        direct[2 * owners + s] = n
        over[s] = (n + 1) >> 1
        over[owners + s] = n - ((n + 1) >> 1)
        return 0

    lax.fori_loop(0, owners, begin, 0)

    def balance(k, _):
        s = k & (owners - 1)
        n = direct[2 * owners + s]
        by_x = jnp.maximum(direct[s] + over[owners + (s ^ 4)], direct[owners + (s ^ 2)] + over[owners + (s ^ 2)])
        by_y = jnp.maximum(direct[owners + s] + over[s ^ 2], direct[s ^ 4] + over[s ^ 4])
        want = (n + by_y - by_x + 1) >> 1
        want = jnp.minimum(jnp.maximum(want, jnp.maximum(n - cap, 0)), jnp.minimum(n, cap))
        over[s] = want
        over[owners + s] = n - want
        return 0

    lax.fori_loop(0, 3 * owners, balance, 0)

    def split(s, _):
        def take(_, carry):
            left, taken = carry
            low = left & -left
            return left ^ low, taken | low

        left, taken = lax.fori_loop(0, over[s], take, (far_of(s), jnp.int32(0)))
        masks[base + s] = taken
        masks[base + owners + s] = left
        return 0

    lax.fori_loop(0, owners, split, 0)

    def longest(s, most_yet):
        for axis, other in ((0, 4), (1, 2)):
            own = direct[axis * owners + s] + over[axis * owners + s]
            passed = over[(1 - axis) * owners + (s ^ other)]
            length = jnp.where(passed > 0, jnp.maximum(own, 2 * LEAD) + passed, own)
            most_yet = jnp.maximum(most_yet, length)
        return most_yet

    length = lax.fori_loop(0, owners, longest, jnp.int32(0))
    total[0] = length

    for axis in range(2):

        def own(at, chip, bit, axis=axis):
            ping = bit & (ping_dev - 1)
            tile = 2 * chip + (bit >> bits)
            send[axis * room + at] = ping
            send[places + axis * room + at] = shifts[tile * pings + me * ping_dev + ping]

        def relay(at, behind, chip, bit, i, axis=axis):
            send[axis * room + at] = ping_dev + i

        link_list(masks, owners, me, axis, own, relay)

    for k, tile in ((0, me), (1, me ^ 1)):

        def mine(j, at, k=k, tile=tile):
            p = fp[tile, j]
            here = (p >> bits) == me

            @pl.when(here)
            def _():
                send[2 * room + k * cap + at] = p & (ping_dev - 1)
                send[places + 2 * room + k * cap + at] = off[tile, j]

            return at + here.astype(jnp.int32)

        lax.fori_loop(0, cnt[tile], mine, jnp.int32(0))


def places_kernel(owners, ping_dev, cap, fp, cnt, masks, shifts, me_ref, _, table):
    bits = ping_dev.bit_length() - 1
    room = 4 * cap
    count = 4 * room + 2 * cap
    pings = owners * ping_dev
    me = me_ref[0]

    def clear(i, _):
        table[i] = 0
        return 0

    lax.fori_loop(0, 3 * count, clear, 0, unroll=12)

    def put(at, tile, ping):
        @pl.when(tile == me)
        def _():
            table[at] = ping
            table[count + at] = shifts[tile * pings + ping]
            table[2 * count + at] = 1

    for a, (axis, flip) in enumerate(((0, 2), (1, 4), (0, 3), (1, 5))):
        s = me ^ flip

        def own(at, chip, bit, a=a, s=s):
            put(a * room + at, 2 * chip + (bit >> bits), s * ping_dev + (bit & (ping_dev - 1)))

        def relay(at, behind, chip, bit, i, a=a):
            put(a * room + at, 2 * chip + (bit >> bits), behind * ping_dev + (bit & (ping_dev - 1)))

        link_list(masks, owners, s, axis, own, relay)

    for k, s in ((0, me), (1, me ^ 1)):

        def listed(j, at, k=k, s=s):
            p = fp[me, j]
            here = (p >> bits) == s

            @pl.when(here)
            def _():
                put(4 * room + k * cap + at, me, p)

            return at + here.astype(jnp.int32)

        lax.fori_loop(0, cnt[me], listed, jnp.int32(0))


def gather_kernel(ping_dev, places, spans, send, echoes, halo, _, *refs):
    outs, stage, sems = refs[-len(spans) - 2 : -2], refs[-2], refs[-1]
    sources = refs[: -len(spans) - 2]
    width = echoes.shape[2]
    blocks = width // LANES
    lane = lax.broadcasted_iota(jnp.int32, (2 * C, LANES), 1)
    jobs = [(begin + i, out, i, axis) for (begin, n, axis), out in zip(spans, outs) for i in range(n)]

    def copies(number):
        at, out, i, axis = jobs[number]
        index = send[at]
        here = jnp.minimum(index, ping_dev - 1)
        plain = [
            pltpu.make_async_copy(echoes.at[here], stage.at[number, :, pl.ds(0, width)], sems.at[number, 0]),
            pltpu.make_async_copy(halo.at[here], stage.at[number, :, pl.ds(width, LANES)], sems.at[number, 1]),
        ]
        if not sources:
            return [(None, plain)]
        groups = [(index < ping_dev, plain)]
        for k in range(len(sources) // 2):
            low = ping_dev + k * LEAD
            chosen = (index >= low) & (index < low + LEAD)
            source = sources[2 * k + 1 - axis].at[jnp.clip(index - low, 0, LEAD - 1)]
            groups.append((chosen, [pltpu.make_async_copy(source, out.at[i], sems.at[number, 0])]))
        return groups

    def act_on(number, act):
        for chosen, group in copies(number):
            if chosen is None:
                for copy in group:
                    act(copy)
            else:

                @pl.when(chosen)
                def _(group=group):
                    for copy in group:
                        act(copy)

    for number in range(len(jobs)):
        act_on(number, lambda copy: copy.start())
    for number in range(len(jobs)):
        act_on(number, lambda copy: copy.wait())

    number = 0
    for (begin, n, _), out in zip(spans, outs):

        def cut(i, _, begin=begin, out=out, number=number):
            offset = send[places + begin + i]
            within = offset & (LANES - 1)
            roll = (LANES - within) & (LANES - 1)
            keep = lane < LANES - within
            low = jnp.where(offset < 0, -LANES, 0)

            def rolled(b):
                start = low + b * LANES
                if b == 0:
                    start = jnp.where(start < 0, width, start)
                span = pl.ds(pl.multiple_of(start, LANES), LANES)
                return pltpu.roll(stage[number + i, :, span].astype(jnp.float32), roll, 1)

            @pl.when(send[begin + i] < ping_dev)
            def _():
                before = rolled(0)
                for b in range(blocks):
                    following = rolled(b + 1)
                    out[i, :, pl.ds(b * LANES, LANES)] = jnp.where(keep, before, following).astype(out.dtype)
                    before = following

            return 0

        lax.fori_loop(0, n, cut, 0)
        number += n


def turned(turn):
    g = turn - jnp.floor(turn + 0.5)
    u = g * g
    cosine = jnp.full_like(u, COS_TERMS[-1])
    for term in COS_TERMS[-2::-1]:
        cosine = cosine * u + term
    sine = jnp.full_like(u, SIN_TERMS[-1])
    for term in SIN_TERMS[-2::-1]:
        sine = sine * u + term
    return cosine, sine * g


def residue(number):
    modulus = jnp.float32(phase_modulus)
    return number - jnp.floor(number * jnp.float32(1.0 / phase_modulus) + 0.5) * modulus


def depths(slots):
    steps = (4, 6, 8, 9, 10, 11, 12)
    return sorted({-(-slots * k // (12 * UNIT)) * UNIT for k in steps})


def depth_of(count, slots):
    return functools.reduce(lambda least, n: jnp.where(count <= n, n, least), reversed(depths(slots)), slots)


def weights_kernel(spacing, pixels, slots, table, where, cnt, me_ref, turn_ref, _, out, mark, chirp, inner, outer, columns, known):
    count = table.shape[0] // 3
    me = me_ref[0]
    step = pl.program_id(0)
    strip = inner.shape[1]
    strips = pixels // strip
    width = out.shape[1]
    inverse = jnp.float32(1.0 / phase_modulus)
    wide = 4 * LANES

    def rows_of(height, across):
        return lax.broadcasted_iota(jnp.int32, (height, across), 0).astype(jnp.float32)

    @pl.when(step == 0)
    def _():
        mark[...] = jnp.zeros_like(mark)
        tall = min(pixels, 256)

        def one_part(r, _):
            start = pl.multiple_of(r * tall, tall)
            x = residue(rows_of(tall, LANES) + start.astype(jnp.float32))
            cosine, sine = turned(residue(x * x) * inverse)
            chirp[0, pl.ds(start, tall), :] = cosine
            chirp[1, pl.ds(start, tall), :] = sine
            return 0

        lax.fori_loop(0, pixels // tall, one_part, 0)
        columns[...] = jnp.zeros_like(columns)
        lane = lax.broadcasted_iota(jnp.int32, (1, LANES), 1)

        def note(i, at):
            live = table[2 * count + where[i]]

            @pl.when(live > 0)
            def _():
                ping = table[where[i]]
                half = (lane >= 2 * C) == ((at & 1) == 1)
                span = pl.ds(pl.multiple_of((at >> 1) * LANES, LANES), LANES)
                distance = (me * pixels - ping * spacing).astype(jnp.float32)
                turn = table[count + where[i]].astype(jnp.float32) * 0.125 - turn_ref[ping]
                for row, value in ((0, distance), (1, turn), (2, jnp.float32(1.0))):
                    columns[row : row + 1, span] = jnp.where(half, value, columns[row : row + 1, span])

            return at + live

        known[0] = lax.fori_loop(0, slots, note, jnp.int32(0))
        amount = jnp.full((1, wide), cnt[me], jnp.int32).astype(jnp.float32)
        root = jnp.sqrt(jnp.float32(C) * amount)
        lane = lax.broadcasted_iota(jnp.int32, (1, wide), 1)
        channel = (lane % C).astype(jnp.float32)
        part = ((lane // C) % 2).astype(jnp.float32)

        def angles(i, _):
            span = pl.ds(pl.multiple_of(i * wide, wide), wide)
            base = residue(columns[0:1, span] - 2.0 * channel)
            cosine, sine = turned(residue(2.0 * rows_of(strip, wide) * base) * inverse)
            inner[0, :, span] = cosine
            inner[1, :, span] = sine
            far = residue(rows_of(strips, wide) * (2.0 * strip))
            angle = residue(residue(far * base) + residue(base * base)) * inverse
            cosine, sine = turned(angle + (columns[1:2, span] + 0.25 * part))
            scale = columns[2:3, span] / root
            outer[0, :, span] = cosine * scale
            outer[1, :, span] = sine * scale
            return 0

        known[0] = depth_of(known[0], whole_units(slots))
        lax.fori_loop(0, (known[0] * 2 * C + wide - 1) // wide, angles, 0)

    @pl.when(STEP * step < known[0])
    def _():
        for pair in range(width // LANES):
            span = pl.ds(pl.multiple_of(step * width + pair * LANES, LANES), LANES)
            column = pl.ds(pair * LANES, LANES)
            inner_real, inner_imag = inner[0, :, span], inner[1, :, span]
            outer_real, outer_imag = outer[0, :, span], outer[1, :, span]
            for s in range(strips):
                real, imag = outer_real[s : s + 1], outer_imag[s : s + 1]
                mid_real = inner_real * real - inner_imag * imag
                mid_imag = inner_real * imag + inner_imag * real
                here = pl.ds(s * strip, strip)
                chirp_real, chirp_imag = chirp[0, here, :], chirp[1, here, :]
                low = pl.ds(pixels + s * strip, strip)
                out[here, column] = (mid_real * chirp_real - mid_imag * chirp_imag).astype(out.dtype)
                out[low, column] = (mid_real * chirp_imag + mid_imag * chirp_real).astype(out.dtype)


def focus_kernel(sizes, table, where, _, weights, *refs):
    arrays = refs[: len(sizes)]
    total, out, mark, window, sems, known = refs[len(sizes) :]
    count = table.shape[0] // 3
    rows = 2 * C
    slots = weights.shape[1] // rows
    column = out.shape[1]
    here = pl.ds(pl.multiple_of(pl.program_id(1) * column, column), column)

    def window_copy(array, i, at):
        place = pl.ds(pl.multiple_of(at * rows, rows), rows)
        return pltpu.make_async_copy(array.at[i], window.at[place, :], sems.at[at])

    @pl.when((pl.program_id(0) == 0) & (pl.program_id(1) == 0))
    def _():
        mark[...] = jnp.zeros_like(mark)
        at, slot = jnp.int32(0), 0
        for array, size in zip(arrays, sizes):
            for i in range(size):
                live = table[2 * count + where[slot]]

                @pl.when(live > 0)
                def _(array=array, i=i, at=at):
                    window_copy(array, i, at).start()

                at, slot = at + live, slot + 1

        def blank(i, _):
            window[pl.ds(pl.multiple_of(i * rows, rows), rows), :] = jnp.zeros((rows, window.shape[1]), window.dtype)
            return 0

        known[0] = depth_of(at, slots)
        lax.fori_loop(at, known[0], blank, 0)

        def ready(i, _):
            window_copy(arrays[0], 0, i).wait()
            return 0

        lax.fori_loop(0, at, ready, 0)

    tall = weights.shape[0]
    piece = min(tall, PIECE)
    for depth in depths(slots):

        @pl.when(known[0] == depth)
        def _(depth=depth):
            deep = pl.ds(0, depth * rows)

            def one_piece(r, _):
                part = pl.ds(pl.multiple_of(r * piece, piece), piece)
                product = jnp.dot(weights[part, deep], window[deep, here], preferred_element_type=jnp.float32)
                out[part, :] = (total[part, :].astype(jnp.float32) + product).astype(out.dtype)
                return 0

            lax.fori_loop(0, tall // piece, one_piece, 0)


def params(mib):
    return pltpu.CompilerParams(vmem_limit_bytes=mib * MIB)


def swap(shard, by):
    return lax.ppermute(shard, "ping", [(i, i ^ by) for i in range(lax.axis_size("ping"))])


def correlated(echoes, pairing, last_ping):
    channel_ids = jnp.arange(C, dtype=jnp.int32)
    front_pick = (pairing[:, 0, :, None] == channel_ids).astype(jnp.bfloat16)
    rear_pick = (pairing[:, 1, :, None] == channel_ids).astype(jnp.bfloat16)
    rear_rows = jnp.einsum("pkc,pzcr->pzkr", rear_pick, echoes, preferred_element_type=jnp.float32)
    inner_rows = jnp.einsum(
        "pkc,pzcr->pzkr", front_pick[1:], echoes[:-1], preferred_element_type=jnp.float32
    )
    lead_rows = jnp.einsum(
        "kc,zcr->zkr", front_pick[0], last_ping, preferred_element_type=jnp.float32
    )
    front_rows = jnp.concatenate([lead_rows[None], inner_rows], axis=0)
    cross_sum = jnp.sum(
        front_rows[:, 0] * rear_rows[:, 1] - front_rows[:, 1] * rear_rows[:, 0], axis=(1, 2)
    )
    front_energy = jnp.sum(front_rows * front_rows, axis=(1, 2, 3))
    rear_energy = jnp.sum(rear_rows * rear_rows, axis=(1, 2, 3))
    return jnp.stack([cross_sum, front_energy, rear_energy])


def over_ranges(parts):
    ranges = lax.axis_size("rng")
    if ranges & (ranges - 1):
        return lax.psum(parts, "rng")
    others = [lax.ppermute(parts, "rng", [(i, i ^ by) for i in range(ranges)]) for by in range(1, ranges)]
    return functools.reduce(jnp.add, others, parts)


def over_chip(parts):
    owners = lax.axis_size("ping")
    mine = jnp.arange(owners, dtype=jnp.int32)[:, None] == lax.axis_index("ping")
    every = jnp.where(mine, parts[:, None, :], 0.0)
    return every + swap(every, 1)


def turns(every):
    every = every + (swap(every, 2) + (swap(every, 4) + swap(every, 6)))
    cross_sum, front_energy, rear_energy = every.reshape(3, -1)
    increment = cross_sum / (jnp.sqrt(front_energy * rear_energy) + small_value)
    order = jnp.arange(increment.shape[0], dtype=jnp.int32)
    track_turn = jnp.sum(jnp.where(order[None, :] <= order[:, None], increment[None, :], 0.0), axis=1)
    turn = track_turn * (1.0 / (2.0 * math.pi))
    return turn - jnp.floor(turn + 0.5)


def gather(send, flat, halo, spans, relayed=(), tie=None):
    ping_dev, channels, width = flat.shape
    total = sum(n for _, n, _ in spans)
    return pl.pallas_call(
        functools.partial(gather_kernel, ping_dev, send.shape[0] // 2, spans),
        out_shape=[jax.ShapeDtypeStruct((n, channels, width), flat.dtype) for _, n, _ in spans],
        in_specs=[SMEM] + [ANY] * (3 + 2 * len(relayed)),
        out_specs=[VMEM] * len(spans),
        scratch_shapes=[
            pltpu.VMEM((total, channels, width + LANES), flat.dtype),
            pltpu.SemaphoreType.DMA((total, 2)),
        ],
        compiler_params=params(16),
        cost_estimate=SMALL,
        name="gather",
    )(send, flat, halo, send if tie is None else tie, *[a for pair in relayed for a in pair])


def whole_units(slots):
    return -(-slots // UNIT) * UNIT


def weights_of(places, table, counts, me, turn, pixels, spacing, tie):
    slots = whole_units(len(places))
    lanes = STEP * 2 * C
    across = -(-slots * 2 * C // (4 * LANES)) * 4 * LANES
    return pl.pallas_call(
        functools.partial(weights_kernel, spacing, pixels, len(places)),
        grid=(slots // STEP,),
        in_specs=[SMEM] * 5 + [ANY],
        out_specs=[pl.BlockSpec((2 * pixels, lanes), lambda i: (0, i)), pl.BlockSpec((8, LANES), lambda i: (0, 0))],
        out_shape=[
            jax.ShapeDtypeStruct((2 * pixels, slots * 2 * C), jnp.bfloat16),
            jax.ShapeDtypeStruct((8, LANES), jnp.float32),
        ],
        scratch_shapes=[
            pltpu.VMEM((2, pixels, LANES), jnp.float32),
            pltpu.VMEM((2, STRIP, across), jnp.float32),
            pltpu.VMEM((2, pixels // STRIP, across), jnp.float32),
            pltpu.VMEM((8, across), jnp.float32),
            pltpu.SMEM((1,), jnp.int32),
        ],
        cost_estimate=SMALL,
        name="weights",
    )(table, np.asarray(places, np.int32), counts, me, turn, tie)


def add_windows(total, arrays, places, weight, table, tie, kind=None):
    height, deep = weight.shape
    width = arrays[0].shape[2]
    flat = pl.BlockSpec((TALL, COLUMN), lambda r, i: (r, i))
    inner = pl.BlockSpec((None, TALL, COLUMN), lambda r, i: (i, r, 0))
    return pl.pallas_call(
        functools.partial(focus_kernel, [a.shape[0] for a in arrays]),
        grid=(height // TALL, width // COLUMN),
        in_specs=[SMEM] * 2
        + [ANY, pl.BlockSpec((TALL, deep), lambda r, i: (r, 0))]
        + [ANY] * len(arrays)
        + [flat if total.ndim == 2 else inner],
        out_specs=[inner if kind is None else flat, pl.BlockSpec((8, LANES), lambda r, i: (0, 0))],
        out_shape=[
            jax.ShapeDtypeStruct((width // COLUMN, height, COLUMN), jnp.float32)
            if kind is None
            else jax.ShapeDtypeStruct((height, width), kind),
            jax.ShapeDtypeStruct((8, LANES), jnp.float32),
        ],
        scratch_shapes=[
            pltpu.VMEM((deep, width), jnp.bfloat16),
            pltpu.SemaphoreType.DMA((deep // (2 * C),)),
            pltpu.SMEM((1,), jnp.int32),
        ],
        compiler_params=params(FOCUS_MIB),
        cost_estimate=SMALL,
        name="focus",
    )(table, np.asarray(places, np.int32), tie, weight, *arrays, total)


def places_of(begin, n, room):
    return [a * room + begin + i for a in range(4) for i in range(n)]


def with_sibling(pair):
    return [pair[0], pair[1], swap(pair[0], 1), swap(pair[1], 1)]


def finished(stage, begin, total, length, flat, halo, send, table, turn, counts, me, over, pixels, spacing, last):
    if stage == len(EXTRA):
        return last(total)
    room = 4 * -(-MOST // lax.axis_size("ping"))

    def more(total):
        at = begin
        for n in EXTRA[stage]:
            cut = gather(send, flat, halo, [(at, n, 0), (room + at, n, 1)], over[:2], table)
            places = places_of(at, n, room)
            weight, _ = weights_of(places, table, counts, me, turn, pixels, spacing, cut[0])
            pair = (swap(cut[0], 2), swap(cut[1], 4))
            total, _ = add_windows(total, with_sibling(pair), places, weight, table, cut[0])
            at += n
        return finished(
            stage + 1, at, total, length, flat, halo, send, table, turn, counts, me, over, pixels, spacing, last
        )

    return lax.cond(length > begin, more, last, total)


def paired_device(echoes, pairing, footprint, counts, offsets, earlier):
    owners, ranges = lax.axis_size("ping"), lax.axis_size("rng")
    tiles = footprint.shape[0]
    ping_dev, _, _, width = echoes.shape
    cap = -(-MOST // owners)
    room = 4 * cap
    base = owners * (owners // 2)
    me = lax.axis_index("ping").astype(jnp.int32).reshape(1)
    whole = lambda *shape: jax.ShapeDtypeStruct(shape, jnp.int32)
    send, masks, shifts, length = pl.pallas_call(
        functools.partial(plan_kernel, owners, ping_dev, cap, tiles),
        out_shape=[
            whole(2 * (2 * room + 2 * cap)), whole(base + 2 * owners), whole(tiles * owners * ping_dev), whole(1)
        ],
        in_specs=[SMEM] * 4,
        out_specs=[SMEM] * 4,
        scratch_shapes=[pltpu.SMEM((3 * owners,), jnp.int32), pltpu.SMEM((2 * owners,), jnp.int32)],
        cost_estimate=SMALL,
        name="plan",
    )(footprint, counts, offsets, me)
    echoes, masks = lax.optimization_barrier((echoes, masks))
    last_ping = passed_along(echoes[-1], "ping", 1)
    flat = echoes.reshape(ping_dev, 2 * C, width)
    head = lax.slice_in_dim(flat, 0, LANES, axis=2)
    tail = lax.slice_in_dim(flat, width - LANES, width, axis=2)
    behind = lax.ppermute(head, "rng", [(i + 1, i) for i in range(ranges - 1)])
    ahead = lax.ppermute(tail, "rng", [(i, i + 1) for i in range(ranges - 1)])
    halo = jnp.where(jnp.arange(LANES) < BAND, behind, ahead)
    parts = correlated(echoes, pairing, last_ping)
    summed = over_ranges(parts)

    def spans_of(c):
        begin = sum(CHUNKS[:c])
        return [(begin, CHUNKS[c], 0), (room + begin, CHUNKS[c], 1)]

    turn = turns(over_chip(summed))
    moved = gather(send, flat, halo, spans_of(0))
    over = [(swap(moved[0], 2), swap(moved[1], 4))]
    own, sibling = gather(send, flat, halo, [(2 * room, cap, None), (2 * room + cap, cap, None)], (), moved[0])
    table = pl.pallas_call(
        functools.partial(places_kernel, owners, ping_dev, cap),
        out_shape=whole(3 * (4 * room + 2 * cap)),
        in_specs=[SMEM] * 5 + [ANY],
        out_specs=SMEM,
        cost_estimate=SMALL,
        name="places",
    )(footprint, counts, masks, shifts, me, own)
    moved = gather(send, flat, halo, spans_of(1), (), table)
    over.append((swap(moved[0], 2), swap(moved[1], 4)))
    pixels = earlier.shape[2]
    spacing = pixels * earlier.shape[0] // ping_dev
    places = [places_of(sum(CHUNKS[:c]), n, room) for c, n in enumerate(CHUNKS)]
    early = [4 * room + i for i in range(2 * cap)] + places[0] + places[1]
    late = places[2] + places[3]
    early_weights, mark = weights_of(early, table, counts, me, turn, pixels, spacing, moved[0])
    over[0], mark = lax.optimization_barrier((over[0], mark))
    arrays = [own, swap(sibling, 1)] + with_sibling(over[0])
    moved = gather(send, flat, halo, spans_of(2), over[:1], mark)
    over.append((swap(moved[0], 2), swap(moved[1], 4)))
    late_weights, mark = weights_of(late, table, counts, me, turn, pixels, spacing, moved[0])
    over[1], mark = lax.optimization_barrier((over[1], mark))
    arrays = arrays + with_sibling(over[1])
    moved = gather(send, flat, halo, spans_of(3), over[:2], mark)
    over.append((swap(moved[0], 2), swap(moved[1], 4)))
    total, mark = add_windows(earlier.reshape(2 * pixels, width), arrays, early, early_weights, table, moved[0])
    over[2], over[3], mark = lax.optimization_barrier((over[2], over[3], mark))
    arrays = with_sibling(over[2]) + with_sibling(over[3])

    def last(total):
        return add_windows(total, arrays, late, late_weights, table, mark, earlier.dtype)[0]

    image = finished(
        0, sum(CHUNKS), total, length[0], flat, halo, send, table, turn, counts, me, over[:2], pixels, spacing, last
    )
    return image.reshape(earlier.shape)


def per_device(echoes, pairing, footprint, counts, offsets, earlier):
    owners = lax.axis_size("ping")
    ping_dev = echoes.shape[0]
    paired = (
        owners == 8
        and footprint.shape[0] == owners
        and ping_dev <= 16
        and ping_dev & (ping_dev - 1) == 0
        and sum(CHUNKS) + sum(map(sum, EXTRA)) >= 4 * -(-MOST // owners)
    )
    device = paired_device if paired else general_device
    return device(echoes, pairing, footprint, counts, offsets, earlier)


def solution(mesh):
    return jax.shard_map(
        per_device,
        mesh=mesh,
        in_specs=(
            P("ping", None, None, "rng"),
            P("ping", None, None),
            P(),
            P(),
            P(),
            P("ping", None, None, "rng"),
        ),
        out_specs=P("ping", None, None, "rng"),
        check_vma=False,
    )
```

```python
import functools
import math

import jax
import jax.numpy as jnp
import numpy as np
from jax import lax
from jax.experimental import pallas as pl
from jax.experimental.pallas import tpu as pltpu
from jax.sharding import PartitionSpec as P

C = 32
X = 1024
BAND = 64
MOST = 48
TILE_DEV = 1
PING_DEV = 16


phase_modulus = 4099
small_value = 1e-06


def passed_along(shard, axis, by):
    length = lax.axis_size(axis)
    pairs = [(i, i + by) for i in range(length) if 0 <= i + by < length]
    return lax.ppermute(shard, axis, pairs)


def prefix(shard, axis, combine, identity):
    length, position = (lax.axis_size(axis), lax.axis_index(axis))
    everything = lax.all_gather(shard, axis)
    start = jnp.broadcast_to(jnp.asarray(identity, shard.dtype), shard.shape)

    def step(k, before):
        reached = k < position
        new = combine(before, everything[k])
        return jnp.where(reached, new, before)

    return lax.fori_loop(0, length, step, start)


def with_halo(cells, sides, width):
    for axis, dim in sides:
        count = lax.axis_size(axis)
        ends = count - 1
        head = lax.slice_in_dim(cells, 0, width, axis=dim)
        tail = lax.slice_in_dim(cells, cells.shape[dim] - width, cells.shape[dim], axis=dim)
        cells = jnp.concatenate(
            [
                lax.ppermute(tail, axis, [(i, (i + 1) % count) for i in range(ends)]),
                cells,
                lax.ppermute(head, axis, [((i + 1) % count, i) for i in range(ends)]),
            ],
            axis=dim,
        )
    return cells


def weight_matrix(tile_id, ping_ids, shift_ids, live_rows, tile_count):
    spacing = TILE_DEV * X // PING_DEV
    column = jnp.arange(ping_ids.shape[0] * 2 * C, dtype=jnp.int32)
    part_of = column // C % 2
    channel = column % C
    ping_cols = jnp.repeat(ping_ids, 2 * C)
    shift_cols = jnp.repeat(shift_ids, 2 * C)
    live_cols = jnp.repeat(live_rows, 2 * C)
    pixels = jnp.arange(X, dtype=jnp.int32)
    offset = tile_id * X - ping_cols * spacing - 2 * channel
    folded = jnp.remainder(pixels[:, None] + offset[None, :], phase_modulus)
    square = jnp.remainder(folded * folded, phase_modulus)
    phases = square.astype(jnp.float32) * (2.0 * math.pi / phase_modulus) + shift_cols.astype(
        jnp.float32
    )[None, :] * (math.pi / 4.0)
    scales = live_cols / jnp.sqrt(jnp.float32(C) * tile_count.astype(jnp.float32))
    cosine = jnp.cos(phases) * scales[None, :]
    sines = jnp.sin(phases) * scales[None, :]
    upper_rows = jnp.where(part_of[None, :] == 0, cosine, -sines)
    lower_rows = jnp.where(part_of[None, :] == 0, sines, cosine)
    return jnp.concatenate([upper_rows, lower_rows], axis=0).astype(jnp.bfloat16)


def focus_tile(received_data, received_labels):
    flat_rows = received_data.reshape((-1,) + received_data.shape[2:])
    flat_labels = received_labels.reshape(-1, 4)
    live_int = (flat_labels[:, 0] >= 0).astype(jnp.int32)
    ping_ids = flat_labels[:, 1]
    shift_ids = flat_labels[:, 2]
    tile_id = flat_labels[0, 3]
    tile_count = jnp.sum(live_int)
    block_len = flat_rows.shape[3]
    weights = weight_matrix(tile_id, ping_ids, shift_ids, live_int.astype(jnp.float32), tile_count)
    product = jnp.dot(weights, flat_rows.reshape(-1, block_len), preferred_element_type=jnp.float32)
    return product.reshape(2, X, block_len)


def focus(received):
    received_data, received_labels = received
    results = [focus_tile(received_data[:, 0], received_labels[:, 0])]
    return jnp.stack(results, axis=0)


def general_device(echoes, pairing, footprint, counts, offsets, earlier):
    ping_dev = echoes.shape[0]
    owners = lax.axis_size("ping")
    own_index = lax.axis_index("ping")
    channel_ids = jnp.arange(C, dtype=jnp.int32)
    front_pick = (pairing[:, 0, :, None] == channel_ids).astype(jnp.bfloat16)
    rear_pick = (pairing[:, 1, :, None] == channel_ids).astype(jnp.bfloat16)
    rear_rows = jnp.einsum("pkc,pzcr->pzkr", rear_pick, echoes, preferred_element_type=jnp.float32)
    inner_rows = jnp.einsum(
        "pkc,pzcr->pzkr", front_pick[1:], echoes[:-1], preferred_element_type=jnp.float32
    )
    last_ping = passed_along(echoes[-1], "ping", 1)
    lead_rows = jnp.einsum(
        "kc,zcr->zkr", front_pick[0], last_ping, preferred_element_type=jnp.float32
    )
    front_rows = jnp.concatenate([lead_rows[None], inner_rows], axis=0)
    cross_sum = jnp.sum(
        front_rows[:, 0] * rear_rows[:, 1] - front_rows[:, 1] * rear_rows[:, 0], axis=(1, 2)
    )
    front_energy = jnp.sum(front_rows * front_rows, axis=(1, 2, 3))
    rear_energy = jnp.sum(rear_rows * rear_rows, axis=(1, 2, 3))
    cross_sum, front_energy, rear_energy = lax.psum((cross_sum, front_energy, rear_energy), "rng")
    increment = cross_sum / (jnp.sqrt(front_energy * rear_energy) + small_value)
    running = jnp.cumsum(increment)
    before_turn = prefix(running[-1], "ping", jnp.add, jnp.float32(0.0))
    track_turn = before_turn + running
    cosine = jnp.cos(track_turn)[:, None, None]
    sines = jnp.sin(track_turn)[:, None, None]
    real_part = echoes[:, 0].astype(jnp.float32)
    imag_part = echoes[:, 1].astype(jnp.float32)
    corrected = jnp.stack(
        [real_part * cosine + imag_part * sines, imag_part * cosine - real_part * sines], axis=1
    ).astype(jnp.bfloat16)
    tile_total = footprint.shape[0]
    slot_cap = -(-MOST // owners)
    positions = jnp.arange(MOST, dtype=jnp.int32)
    in_list = positions[None, :] < counts[:, None]
    from_here = in_list & (footprint // ping_dev == own_index)
    order_here = jnp.cumsum(from_here.astype(jnp.int32), axis=1) - 1
    slot_ids = jnp.arange(slot_cap, dtype=jnp.int32)
    select = (from_here[:, None, :] & (order_here[:, None, :] == slot_ids[None, :, None])).astype(
        jnp.int32
    )
    place_ids = jnp.sum(select * (positions + 1)[None, None, :], axis=2) - 1
    local_ids = jnp.sum(select * (footprint % ping_dev)[:, None, :], axis=2)
    ping_ids = jnp.sum(select * footprint[:, None, :], axis=2)
    shift_ids = jnp.sum(select * offsets[:, None, :], axis=2)
    tile_ids = jnp.broadcast_to(jnp.arange(tile_total, dtype=jnp.int32)[:, None], place_ids.shape)
    labels = jnp.stack([place_ids, ping_ids, shift_ids, tile_ids], axis=2).reshape(
        owners, tile_total // owners, slot_cap, 4
    )
    block_len = corrected.shape[3]
    source = with_halo(corrected, (("rng", 3),), BAND)

    def cut_window(local_one, offset_one):
        return lax.dynamic_slice(
            source, (local_one, 0, 0, BAND + offset_one), (1, 2, C, block_len)
        )[0]

    outgoing = jax.vmap(cut_window)(local_ids.reshape(-1), shift_ids.reshape(-1))
    outgoing = outgoing.reshape((owners, tile_total // owners, slot_cap, 2, C, block_len))
    contribution = focus(
        (
            lax.all_to_all(outgoing, "ping", split_axis=0, concat_axis=0, tiled=True),
            lax.all_to_all(labels, "ping", split_axis=0, concat_axis=0, tiled=True),
        )
    )
    return (earlier.astype(jnp.float32) + contribution).astype(jnp.bfloat16)


LEAD = 4
CHUNKS = (4, 4, 4, 2)
EXTRA = ((2,), (4, 4))
UNIT = 4
STRIP = 64
STEP = 2 * UNIT
LANES = 128
SMALL = pl.CostEstimate(flops=1024, bytes_accessed=1024, transcendentals=0)
MIB = 1 << 20
COLUMN = 2048
PIECE = 512
TALL = 512
FOCUS_MIB = 56
SMEM = pl.BlockSpec(memory_space=pltpu.SMEM)
ANY = pl.BlockSpec(memory_space=pl.ANY)
VMEM = pl.BlockSpec(memory_space=pltpu.VMEM)
COS_TERMS = (
    1.0, -19.73920440673828, 64.93911743164062, -85.45014190673828, 60.16762924194336,
    -25.967599868774414, 6.528658390045166,
)
SIN_TERMS = (
    6.2831854820251465, -41.34170150756836, 81.60513305664062, -76.70301818847656, 42.02592849731445,
    -14.899847030639648, 3.2381374835968018,
)


def bit_count(mask):
    down = lax.shift_right_logical
    mask = mask - (down(mask, 1) & 0x55555555)
    mask = (mask & 0x33333333) + (down(mask, 2) & 0x33333333)
    mask = (mask + down(mask, 4)) & 0x0F0F0F0F
    mask = mask + down(mask, 8)
    return (mask + down(mask, 16)) & 0x3F


def each_bit(mask, place, visit):
    def body(_, carry):
        left, at = carry
        low = left & -left
        visit(at, bit_count(low - 1))
        return left ^ low, at + 1

    return lax.fori_loop(0, bit_count(mask), body, (mask, place))[1]


def link_list(masks, owners, s, axis, own, relay):
    chips = owners // 2
    near, other = (1, 4) if axis == 0 else (2, 2)
    base = owners * chips
    chip = s >> 1
    behind = s ^ other
    place = each_bit(masks[base + axis * owners + s], jnp.int32(0), lambda at, bit: own(at, chip ^ 3, bit))
    place = each_bit(masks[s * chips + (chip ^ near)], place, lambda at, bit: own(at, chip ^ near, bit))
    begin = jnp.maximum(place, 2 * LEAD)
    passed = masks[base + (1 - axis) * owners + behind]
    each_bit(passed, begin, lambda at, bit: relay(at, behind, chip ^ near, bit, at - begin))


def plan_kernel(owners, ping_dev, cap, tiles, fp, cnt, off, me_ref, send, masks, shifts, total, direct, over):
    chips = owners // 2
    bits = ping_dev.bit_length() - 1
    room = 4 * cap
    base = owners * chips
    pings = owners * ping_dev
    places = 2 * room + 2 * cap
    me = me_ref[0]

    def clear(i, _):
        masks[i] = 0
        return 0

    lax.fori_loop(0, base, clear, 0, unroll=8)

    def clear_send(i, _):
        send[i] = 0
        return 0

    lax.fori_loop(0, 2 * places, clear_send, 0, unroll=12)

    def one_tile(t, _):
        def entry(j, _):
            p = fp[t, j]
            at = (p >> bits) * chips + (t >> 1)
            masks[at] = masks[at] | lax.shift_left(jnp.int32(1), (p & (ping_dev - 1)) + (t & 1) * ping_dev)
            shifts[t * pings + p] = off[t, j]
            return 0

        return lax.fori_loop(0, cnt[t], entry, 0)

    lax.fori_loop(0, tiles, one_tile, 0)

    def far_of(s):
        return masks[s * chips + ((s >> 1) ^ 3)]

    def near_count(s, near):
        return bit_count(masks[s * chips + ((s >> 1) ^ near)])

    def begin(s, _):
        n = bit_count(far_of(s))
        direct[s] = near_count(s, 1)
        direct[owners + s] = near_count(s, 2)
        direct[2 * owners + s] = n
        over[s] = (n + 1) >> 1
        over[owners + s] = n - ((n + 1) >> 1)
        return 0

    lax.fori_loop(0, owners, begin, 0)

    def balance(k, _):
        s = k & (owners - 1)
        n = direct[2 * owners + s]
        by_x = jnp.maximum(direct[s] + over[owners + (s ^ 4)], direct[owners + (s ^ 2)] + over[owners + (s ^ 2)])
        by_y = jnp.maximum(direct[owners + s] + over[s ^ 2], direct[s ^ 4] + over[s ^ 4])
        want = (n + by_y - by_x + 1) >> 1
        want = jnp.minimum(jnp.maximum(want, jnp.maximum(n - cap, 0)), jnp.minimum(n, cap))
        over[s] = want
        over[owners + s] = n - want
        return 0

    lax.fori_loop(0, 3 * owners, balance, 0)

    def split(s, _):
        def take(_, carry):
            left, taken = carry
            low = left & -left
            return left ^ low, taken | low

        left, taken = lax.fori_loop(0, over[s], take, (far_of(s), jnp.int32(0)))
        masks[base + s] = taken
        masks[base + owners + s] = left
        return 0

    lax.fori_loop(0, owners, split, 0)

    def longest(s, most_yet):
        for axis, other in ((0, 4), (1, 2)):
            own = direct[axis * owners + s] + over[axis * owners + s]
            passed = over[(1 - axis) * owners + (s ^ other)]
            length = jnp.where(passed > 0, jnp.maximum(own, 2 * LEAD) + passed, own)
            most_yet = jnp.maximum(most_yet, length)
        return most_yet

    length = lax.fori_loop(0, owners, longest, jnp.int32(0))
    total[0] = length

    for axis in range(2):

        def own(at, chip, bit, axis=axis):
            ping = bit & (ping_dev - 1)
            tile = 2 * chip + (bit >> bits)
            send[axis * room + at] = ping
            send[places + axis * room + at] = shifts[tile * pings + me * ping_dev + ping]

        def relay(at, behind, chip, bit, i, axis=axis):
            send[axis * room + at] = ping_dev + i

        link_list(masks, owners, me, axis, own, relay)

    for k, tile in ((0, me), (1, me ^ 1)):

        def mine(j, at, k=k, tile=tile):
            p = fp[tile, j]
            here = (p >> bits) == me

            @pl.when(here)
            def _():
                send[2 * room + k * cap + at] = p & (ping_dev - 1)
                send[places + 2 * room + k * cap + at] = off[tile, j]

            return at + here.astype(jnp.int32)

        lax.fori_loop(0, cnt[tile], mine, jnp.int32(0))


def places_kernel(owners, ping_dev, cap, fp, cnt, masks, shifts, me_ref, _, table):
    bits = ping_dev.bit_length() - 1
    room = 4 * cap
    count = 4 * room + 2 * cap
    pings = owners * ping_dev
    me = me_ref[0]

    def clear(i, _):
        table[i] = 0
        return 0

    lax.fori_loop(0, 3 * count, clear, 0, unroll=12)

    def put(at, tile, ping):
        @pl.when(tile == me)
        def _():
            table[at] = ping
            table[count + at] = shifts[tile * pings + ping]
            table[2 * count + at] = 1

    for a, (axis, flip) in enumerate(((0, 2), (1, 4), (0, 3), (1, 5))):
        s = me ^ flip

        def own(at, chip, bit, a=a, s=s):
            put(a * room + at, 2 * chip + (bit >> bits), s * ping_dev + (bit & (ping_dev - 1)))

        def relay(at, behind, chip, bit, i, a=a):
            put(a * room + at, 2 * chip + (bit >> bits), behind * ping_dev + (bit & (ping_dev - 1)))

        link_list(masks, owners, s, axis, own, relay)

    for k, s in ((0, me), (1, me ^ 1)):

        def listed(j, at, k=k, s=s):
            p = fp[me, j]
            here = (p >> bits) == s

            @pl.when(here)
            def _():
                put(4 * room + k * cap + at, me, p)

            return at + here.astype(jnp.int32)

        lax.fori_loop(0, cnt[me], listed, jnp.int32(0))


def gather_kernel(ping_dev, places, spans, send, echoes, halo, _, *refs):
    outs, stage, sems = refs[-len(spans) - 2 : -2], refs[-2], refs[-1]
    sources = refs[: -len(spans) - 2]
    width = echoes.shape[2]
    blocks = width // LANES
    lane = lax.broadcasted_iota(jnp.int32, (2 * C, LANES), 1)
    jobs = [(begin + i, out, i, axis) for (begin, n, axis), out in zip(spans, outs) for i in range(n)]

    def copies(number):
        at, out, i, axis = jobs[number]
        index = send[at]
        here = jnp.minimum(index, ping_dev - 1)
        plain = [
            pltpu.make_async_copy(echoes.at[here], stage.at[number, :, pl.ds(0, width)], sems.at[number, 0]),
            pltpu.make_async_copy(halo.at[here], stage.at[number, :, pl.ds(width, LANES)], sems.at[number, 1]),
        ]
        if not sources:
            return [(None, plain)]
        groups = [(index < ping_dev, plain)]
        for k in range(len(sources) // 2):
            low = ping_dev + k * LEAD
            chosen = (index >= low) & (index < low + LEAD)
            source = sources[2 * k + 1 - axis].at[jnp.clip(index - low, 0, LEAD - 1)]
            groups.append((chosen, [pltpu.make_async_copy(source, out.at[i], sems.at[number, 0])]))
        return groups

    def act_on(number, act):
        for chosen, group in copies(number):
            if chosen is None:
                for copy in group:
                    act(copy)
            else:

                @pl.when(chosen)
                def _(group=group):
                    for copy in group:
                        act(copy)

    for number in range(len(jobs)):
        act_on(number, lambda copy: copy.start())
    for number in range(len(jobs)):
        act_on(number, lambda copy: copy.wait())

    number = 0
    for (begin, n, _), out in zip(spans, outs):

        def cut(i, _, begin=begin, out=out, number=number):
            offset = send[places + begin + i]
            within = offset & (LANES - 1)
            roll = (LANES - within) & (LANES - 1)
            keep = lane < LANES - within
            low = jnp.where(offset < 0, -LANES, 0)

            def rolled(b):
                start = low + b * LANES
                if b == 0:
                    start = jnp.where(start < 0, width, start)
                span = pl.ds(pl.multiple_of(start, LANES), LANES)
                return pltpu.roll(stage[number + i, :, span].astype(jnp.float32), roll, 1)

            @pl.when(send[begin + i] < ping_dev)
            def _():
                before = rolled(0)
                for b in range(blocks):
                    following = rolled(b + 1)
                    out[i, :, pl.ds(b * LANES, LANES)] = jnp.where(keep, before, following).astype(out.dtype)
                    before = following

            return 0

        lax.fori_loop(0, n, cut, 0)
        number += n


def turned(turn):
    g = turn - jnp.floor(turn + 0.5)
    u = g * g
    cosine = jnp.full_like(u, COS_TERMS[-1])
    for term in COS_TERMS[-2::-1]:
        cosine = cosine * u + term
    sine = jnp.full_like(u, SIN_TERMS[-1])
    for term in SIN_TERMS[-2::-1]:
        sine = sine * u + term
    return cosine, sine * g


def residue(number):
    modulus = jnp.float32(phase_modulus)
    return number - jnp.floor(number * jnp.float32(1.0 / phase_modulus) + 0.5) * modulus


def depths(slots):
    steps = (4, 6, 8, 9, 10, 11, 12)
    return sorted({-(-slots * k // (12 * UNIT)) * UNIT for k in steps})


def depth_of(count, slots):
    return functools.reduce(lambda least, n: jnp.where(count <= n, n, least), reversed(depths(slots)), slots)


def weights_kernel(spacing, pixels, slots, table, where, cnt, me_ref, turn_ref, _, out, mark, chirp, inner, outer, columns, known):
    count = table.shape[0] // 3
    me = me_ref[0]
    step = pl.program_id(0)
    strip = inner.shape[1]
    strips = pixels // strip
    width = out.shape[1]
    inverse = jnp.float32(1.0 / phase_modulus)
    wide = 4 * LANES

    def rows_of(height, across):
        return lax.broadcasted_iota(jnp.int32, (height, across), 0).astype(jnp.float32)

    @pl.when(step == 0)
    def _():
        mark[...] = jnp.zeros_like(mark)
        tall = min(pixels, 256)

        def one_part(r, _):
            start = pl.multiple_of(r * tall, tall)
            x = residue(rows_of(tall, LANES) + start.astype(jnp.float32))
            cosine, sine = turned(residue(x * x) * inverse)
            chirp[0, pl.ds(start, tall), :] = cosine
            chirp[1, pl.ds(start, tall), :] = sine
            return 0

        lax.fori_loop(0, pixels // tall, one_part, 0)
        columns[...] = jnp.zeros_like(columns)
        lane = lax.broadcasted_iota(jnp.int32, (1, LANES), 1)

        def note(i, at):
            live = table[2 * count + where[i]]

            @pl.when(live > 0)
            def _():
                ping = table[where[i]]
                half = (lane >= 2 * C) == ((at & 1) == 1)
                span = pl.ds(pl.multiple_of((at >> 1) * LANES, LANES), LANES)
                distance = (me * pixels - ping * spacing).astype(jnp.float32)
                turn = table[count + where[i]].astype(jnp.float32) * 0.125 - turn_ref[ping]
                for row, value in ((0, distance), (1, turn), (2, jnp.float32(1.0))):
                    columns[row : row + 1, span] = jnp.where(half, value, columns[row : row + 1, span])

            return at + live

        known[0] = lax.fori_loop(0, slots, note, jnp.int32(0))
        amount = jnp.full((1, wide), cnt[me], jnp.int32).astype(jnp.float32)
        root = jnp.sqrt(jnp.float32(C) * amount)
        lane = lax.broadcasted_iota(jnp.int32, (1, wide), 1)
        channel = (lane % C).astype(jnp.float32)
        part = ((lane // C) % 2).astype(jnp.float32)

        def angles(i, _):
            span = pl.ds(pl.multiple_of(i * wide, wide), wide)
            base = residue(columns[0:1, span] - 2.0 * channel)
            cosine, sine = turned(residue(2.0 * rows_of(strip, wide) * base) * inverse)
            inner[0, :, span] = cosine
            inner[1, :, span] = sine
            far = residue(rows_of(strips, wide) * (2.0 * strip))
            angle = residue(residue(far * base) + residue(base * base)) * inverse
            cosine, sine = turned(angle + (columns[1:2, span] + 0.25 * part))
            scale = columns[2:3, span] / root
            outer[0, :, span] = cosine * scale
            outer[1, :, span] = sine * scale
            return 0

        known[0] = depth_of(known[0], whole_units(slots))
        lax.fori_loop(0, (known[0] * 2 * C + wide - 1) // wide, angles, 0)

    @pl.when(STEP * step < known[0])
    def _():
        for pair in range(width // LANES):
            span = pl.ds(pl.multiple_of(step * width + pair * LANES, LANES), LANES)
            column = pl.ds(pair * LANES, LANES)
            inner_real, inner_imag = inner[0, :, span], inner[1, :, span]
            outer_real, outer_imag = outer[0, :, span], outer[1, :, span]
            for s in range(strips):
                real, imag = outer_real[s : s + 1], outer_imag[s : s + 1]
                mid_real = inner_real * real - inner_imag * imag
                mid_imag = inner_real * imag + inner_imag * real
                here = pl.ds(s * strip, strip)
                chirp_real, chirp_imag = chirp[0, here, :], chirp[1, here, :]
                low = pl.ds(pixels + s * strip, strip)
                out[here, column] = (mid_real * chirp_real - mid_imag * chirp_imag).astype(out.dtype)
                out[low, column] = (mid_real * chirp_imag + mid_imag * chirp_real).astype(out.dtype)


def focus_kernel(sizes, table, where, _, weights, *refs):
    arrays = refs[: len(sizes)]
    total, out, mark, window, sems, known = refs[len(sizes) :]
    count = table.shape[0] // 3
    rows = 2 * C
    slots = weights.shape[1] // rows
    column = out.shape[1]
    here = pl.ds(pl.multiple_of(pl.program_id(1) * column, column), column)

    def window_copy(array, i, at):
        place = pl.ds(pl.multiple_of(at * rows, rows), rows)
        return pltpu.make_async_copy(array.at[i], window.at[place, :], sems.at[at])

    @pl.when((pl.program_id(0) == 0) & (pl.program_id(1) == 0))
    def _():
        mark[...] = jnp.zeros_like(mark)
        at, slot = jnp.int32(0), 0
        for array, size in zip(arrays, sizes):
            for i in range(size):
                live = table[2 * count + where[slot]]

                @pl.when(live > 0)
                def _(array=array, i=i, at=at):
                    window_copy(array, i, at).start()

                at, slot = at + live, slot + 1

        def blank(i, _):
            window[pl.ds(pl.multiple_of(i * rows, rows), rows), :] = jnp.zeros((rows, window.shape[1]), window.dtype)
            return 0

        known[0] = depth_of(at, slots)
        lax.fori_loop(at, known[0], blank, 0)

        def ready(i, _):
            window_copy(arrays[0], 0, i).wait()
            return 0

        lax.fori_loop(0, at, ready, 0)

    tall = weights.shape[0]
    piece = min(tall, PIECE)
    for depth in depths(slots):

        @pl.when(known[0] == depth)
        def _(depth=depth):
            deep = pl.ds(0, depth * rows)

            def one_piece(r, _):
                part = pl.ds(pl.multiple_of(r * piece, piece), piece)
                product = jnp.dot(weights[part, deep], window[deep, here], preferred_element_type=jnp.float32)
                out[part, :] = (total[part, :].astype(jnp.float32) + product).astype(out.dtype)
                return 0

            lax.fori_loop(0, tall // piece, one_piece, 0)


def params(mib):
    return pltpu.CompilerParams(vmem_limit_bytes=mib * MIB)


def swap(shard, by):
    return lax.ppermute(shard, "ping", [(i, i ^ by) for i in range(lax.axis_size("ping"))])


def correlated(echoes, pairing, last_ping):
    channel_ids = jnp.arange(C, dtype=jnp.int32)
    front_pick = (pairing[:, 0, :, None] == channel_ids).astype(jnp.bfloat16)
    rear_pick = (pairing[:, 1, :, None] == channel_ids).astype(jnp.bfloat16)
    rear_rows = jnp.einsum("pkc,pzcr->pzkr", rear_pick, echoes, preferred_element_type=jnp.float32)
    inner_rows = jnp.einsum(
        "pkc,pzcr->pzkr", front_pick[1:], echoes[:-1], preferred_element_type=jnp.float32
    )
    lead_rows = jnp.einsum(
        "kc,zcr->zkr", front_pick[0], last_ping, preferred_element_type=jnp.float32
    )
    front_rows = jnp.concatenate([lead_rows[None], inner_rows], axis=0)
    cross_sum = jnp.sum(
        front_rows[:, 0] * rear_rows[:, 1] - front_rows[:, 1] * rear_rows[:, 0], axis=(1, 2)
    )
    front_energy = jnp.sum(front_rows * front_rows, axis=(1, 2, 3))
    rear_energy = jnp.sum(rear_rows * rear_rows, axis=(1, 2, 3))
    return jnp.stack([cross_sum, front_energy, rear_energy])


def over_ranges(parts):
    ranges = lax.axis_size("rng")
    if ranges & (ranges - 1):
        return lax.psum(parts, "rng")
    others = [lax.ppermute(parts, "rng", [(i, i ^ by) for i in range(ranges)]) for by in range(1, ranges)]
    return functools.reduce(jnp.add, others, parts)


def over_chip(parts):
    owners = lax.axis_size("ping")
    mine = jnp.arange(owners, dtype=jnp.int32)[:, None] == lax.axis_index("ping")
    every = jnp.where(mine, parts[:, None, :], 0.0)
    return every + swap(every, 1)


def turns(every):
    every = every + (swap(every, 2) + (swap(every, 4) + swap(every, 6)))
    cross_sum, front_energy, rear_energy = every.reshape(3, -1)
    increment = cross_sum / (jnp.sqrt(front_energy * rear_energy) + small_value)
    order = jnp.arange(increment.shape[0], dtype=jnp.int32)
    track_turn = jnp.sum(jnp.where(order[None, :] <= order[:, None], increment[None, :], 0.0), axis=1)
    turn = track_turn * (1.0 / (2.0 * math.pi))
    return turn - jnp.floor(turn + 0.5)


def gather(send, flat, halo, spans, relayed=(), tie=None):
    ping_dev, channels, width = flat.shape
    total = sum(n for _, n, _ in spans)
    return pl.pallas_call(
        functools.partial(gather_kernel, ping_dev, send.shape[0] // 2, spans),
        out_shape=[jax.ShapeDtypeStruct((n, channels, width), flat.dtype) for _, n, _ in spans],
        in_specs=[SMEM] + [ANY] * (3 + 2 * len(relayed)),
        out_specs=[VMEM] * len(spans),
        scratch_shapes=[
            pltpu.VMEM((total, channels, width + LANES), flat.dtype),
            pltpu.SemaphoreType.DMA((total, 2)),
        ],
        compiler_params=params(16),
        cost_estimate=SMALL,
        name="gather",
    )(send, flat, halo, send if tie is None else tie, *[a for pair in relayed for a in pair])


def whole_units(slots):
    return -(-slots // UNIT) * UNIT


def weights_of(places, table, counts, me, turn, pixels, spacing, tie):
    slots = whole_units(len(places))
    lanes = STEP * 2 * C
    across = -(-slots * 2 * C // (4 * LANES)) * 4 * LANES
    return pl.pallas_call(
        functools.partial(weights_kernel, spacing, pixels, len(places)),
        grid=(-(-slots // STEP),),
        in_specs=[SMEM] * 5 + [ANY],
        out_specs=[pl.BlockSpec((2 * pixels, lanes), lambda i: (0, i)), pl.BlockSpec((8, LANES), lambda i: (0, 0))],
        out_shape=[
            jax.ShapeDtypeStruct((2 * pixels, slots * 2 * C), jnp.bfloat16),
            jax.ShapeDtypeStruct((8, LANES), jnp.float32),
        ],
        scratch_shapes=[
            pltpu.VMEM((2, pixels, LANES), jnp.float32),
            pltpu.VMEM((2, STRIP, across), jnp.float32),
            pltpu.VMEM((2, pixels // STRIP, across), jnp.float32),
            pltpu.VMEM((8, across), jnp.float32),
            pltpu.SMEM((1,), jnp.int32),
        ],
        cost_estimate=SMALL,
        name="weights",
    )(table, np.asarray(places, np.int32), counts, me, turn, tie)


def add_windows(total, arrays, places, weight, table, tie, kind=None):
    height, deep = weight.shape
    width = arrays[0].shape[2]
    flat = pl.BlockSpec((TALL, COLUMN), lambda r, i: (r, i))
    inner = pl.BlockSpec((None, TALL, COLUMN), lambda r, i: (i, r, 0))
    return pl.pallas_call(
        functools.partial(focus_kernel, [a.shape[0] for a in arrays]),
        grid=(height // TALL, width // COLUMN),
        in_specs=[SMEM] * 2
        + [ANY, pl.BlockSpec((TALL, deep), lambda r, i: (r, 0))]
        + [ANY] * len(arrays)
        + [flat if total.ndim == 2 else inner],
        out_specs=[inner if kind is None else flat, pl.BlockSpec((8, LANES), lambda r, i: (0, 0))],
        out_shape=[
            jax.ShapeDtypeStruct((width // COLUMN, height, COLUMN), jnp.float32)
            if kind is None
            else jax.ShapeDtypeStruct((height, width), kind),
            jax.ShapeDtypeStruct((8, LANES), jnp.float32),
        ],
        scratch_shapes=[
            pltpu.VMEM((deep, width), jnp.bfloat16),
            pltpu.SemaphoreType.DMA((deep // (2 * C),)),
            pltpu.SMEM((1,), jnp.int32),
        ],
        compiler_params=params(FOCUS_MIB),
        cost_estimate=SMALL,
        name="focus",
    )(table, np.asarray(places, np.int32), tie, weight, *arrays, total)


def places_of(begin, n, room):
    return [a * room + begin + i for a in range(4) for i in range(n)]


def with_sibling(pair):
    return [pair[0], pair[1], swap(pair[0], 1), swap(pair[1], 1)]


def finished(stage, begin, total, length, flat, halo, send, table, turn, counts, me, over, pixels, spacing, last):
    if stage == len(EXTRA):
        return last(total)
    room = 4 * -(-MOST // lax.axis_size("ping"))

    def more(total):
        at = begin
        for n in EXTRA[stage]:
            cut = gather(send, flat, halo, [(at, n, 0), (room + at, n, 1)], over[:2], table)
            places = places_of(at, n, room)
            weight, _ = weights_of(places, table, counts, me, turn, pixels, spacing, cut[0])
            pair = (swap(cut[0], 2), swap(cut[1], 4))
            total, _ = add_windows(total, with_sibling(pair), places, weight, table, cut[0])
            at += n
        return finished(
            stage + 1, at, total, length, flat, halo, send, table, turn, counts, me, over, pixels, spacing, last
        )

    return lax.cond(length > begin, more, last, total)


def paired_device(echoes, pairing, footprint, counts, offsets, earlier):
    owners, ranges = lax.axis_size("ping"), lax.axis_size("rng")
    tiles = footprint.shape[0]
    ping_dev, _, _, width = echoes.shape
    cap = -(-MOST // owners)
    room = 4 * cap
    base = owners * (owners // 2)
    me = lax.axis_index("ping").astype(jnp.int32).reshape(1)
    whole = lambda *shape: jax.ShapeDtypeStruct(shape, jnp.int32)
    send, masks, shifts, length = pl.pallas_call(
        functools.partial(plan_kernel, owners, ping_dev, cap, tiles),
        out_shape=[
            whole(2 * (2 * room + 2 * cap)), whole(base + 2 * owners), whole(tiles * owners * ping_dev), whole(1)
        ],
        in_specs=[SMEM] * 4,
        out_specs=[SMEM] * 4,
        scratch_shapes=[pltpu.SMEM((3 * owners,), jnp.int32), pltpu.SMEM((2 * owners,), jnp.int32)],
        cost_estimate=SMALL,
        name="plan",
    )(footprint, counts, offsets, me)
    echoes, masks = lax.optimization_barrier((echoes, masks))
    last_ping = passed_along(echoes[-1], "ping", 1)
    flat = echoes.reshape(ping_dev, 2 * C, width)
    head = lax.slice_in_dim(flat, 0, LANES, axis=2)
    tail = lax.slice_in_dim(flat, width - LANES, width, axis=2)
    behind = lax.ppermute(head, "rng", [(i + 1, i) for i in range(ranges - 1)])
    ahead = lax.ppermute(tail, "rng", [(i, i + 1) for i in range(ranges - 1)])
    halo = jnp.where(jnp.arange(LANES) < BAND, behind, ahead)
    parts = correlated(echoes, pairing, last_ping)
    summed = over_ranges(parts)

    def spans_of(c):
        begin = sum(CHUNKS[:c])
        return [(begin, CHUNKS[c], 0), (room + begin, CHUNKS[c], 1)]

    turn = turns(over_chip(summed))
    moved = gather(send, flat, halo, spans_of(0))
    over = [(swap(moved[0], 2), swap(moved[1], 4))]
    own, sibling = gather(send, flat, halo, [(2 * room, cap, None), (2 * room + cap, cap, None)], (), moved[0])
    table = pl.pallas_call(
        functools.partial(places_kernel, owners, ping_dev, cap),
        out_shape=whole(3 * (4 * room + 2 * cap)),
        in_specs=[SMEM] * 5 + [ANY],
        out_specs=SMEM,
        cost_estimate=SMALL,
        name="places",
    )(footprint, counts, masks, shifts, me, own)
    moved = gather(send, flat, halo, spans_of(1), (), table)
    over.append((swap(moved[0], 2), swap(moved[1], 4)))
    pixels = earlier.shape[2]
    spacing = pixels * earlier.shape[0] // ping_dev
    places = [places_of(sum(CHUNKS[:c]), n, room) for c, n in enumerate(CHUNKS)]
    early = [4 * room + i for i in range(2 * cap)] + places[0] + places[1]
    late = places[2] + places[3]
    early_weights, mark = weights_of(early, table, counts, me, turn, pixels, spacing, moved[0])
    over[0], mark = lax.optimization_barrier((over[0], mark))
    arrays = [own, swap(sibling, 1)] + with_sibling(over[0])
    moved = gather(send, flat, halo, spans_of(2), over[:1], mark)
    over.append((swap(moved[0], 2), swap(moved[1], 4)))
    late_weights, mark = weights_of(late, table, counts, me, turn, pixels, spacing, moved[0])
    over[1], mark = lax.optimization_barrier((over[1], mark))
    arrays = arrays + with_sibling(over[1])
    moved = gather(send, flat, halo, spans_of(3), over[:2], mark)
    over.append((swap(moved[0], 2), swap(moved[1], 4)))
    total, mark = add_windows(earlier.reshape(2 * pixels, width), arrays, early, early_weights, table, moved[0])
    over[2], over[3], mark = lax.optimization_barrier((over[2], over[3], mark))
    arrays = with_sibling(over[2]) + with_sibling(over[3])

    def last(total):
        return add_windows(total, arrays, late, late_weights, table, mark, earlier.dtype)[0]

    image = finished(
        0, sum(CHUNKS), total, length[0], flat, halo, send, table, turn, counts, me, over[:2], pixels, spacing, last
    )
    return image.reshape(earlier.shape)


def per_device(echoes, pairing, footprint, counts, offsets, earlier):
    owners = lax.axis_size("ping")
    ping_dev = echoes.shape[0]
    paired = (
        owners == 8
        and footprint.shape[0] == owners
        and ping_dev <= 16
        and ping_dev & (ping_dev - 1) == 0
        and sum(CHUNKS) + sum(map(sum, EXTRA)) >= 4 * -(-MOST // owners)
    )
    device = paired_device if paired else general_device
    return device(echoes, pairing, footprint, counts, offsets, earlier)


def solution(mesh):
    return jax.shard_map(
        per_device,
        mesh=mesh,
        in_specs=(
            P("ping", None, None, "rng"),
            P("ping", None, None),
            P(),
            P(),
            P(),
            P("ping", None, None, "rng"),
        ),
        out_specs=P("ping", None, None, "rng"),
        check_vma=False,
    )
```
